256 devices in a mesh: frames: 64 (over x, z, core), mp: 4 (over y).
Axes of the slice: x: 4, y: 4, z: 8, core: 2. Of those that a mesh axis runs over, the one named last changes fastest.
Arguments:
- frames_in: bfloat16 [256, 16, 32, 768], P('frames'), may hold values from -6 to 6
- fine_gain: float32 [768], replicated, may hold values from 0.1 to 1.9
- fine_query_key_value: bfloat16 [768, 3, 768], P(None, None, 'mp'), may hold values from -64 to 64
- fine_out: bfloat16 [768, 768], P('mp'), may hold values from -1.25 to 1.25
- merge_weight: bfloat16 [768, 1536], replicated, may hold values from -0.875 to 0.875
- coarse_gain: float32 [1536], replicated, may hold values from 0.1 to 1.9
- coarse_query_key_value: bfloat16 [1536, 3, 1536], P(None, None, 'mp'), may hold values from -64 to 64
- coarse_out: bfloat16 [1536, 1536], P('mp'), may hold values from -12 to 12
- split_weight: bfloat16 [1536, 768], P(None, 'mp'), may hold values from -0.15625 to 0.15625
Outputs:
- frames_out: bfloat16 [256, 16, 32, 768], P('frames', None, None, 'mp')
The draws below stay inside these ranges and needn't reach their ends.
All inputs are finite; a program needn't handle non-finite values.
Results may differ from the reference program's by a relative error of at most 0.04.
Values may be sent and summed in bfloat16 or wider, within the bound.
No kernel may reach another device: no remote copies, remote signals or barrier semaphores. Data moves between devices by JAX's collectives and lax.ppermute only.
A program may use at most 128 MiB of HBM per device.

```python
import jax
import jax.numpy as jnp
from jax import lax

D = 768
DC = 1536
HEADS = 12
ROWS = 16
COLS = 32
CLIP_FRAME_COUNT = 256


def draw_fine_query_key_value(key, part):
    key = jax.random.fold_in(key, 11)
    projection = jnp.clip(jax.random.normal(jax.random.fold_in(key, 1), (D, 3, D), jnp.float32), -6.0, 6.0) * D ** (-0.5)
    return projection.astype(jnp.bfloat16)


def draw_coarse_query_key_value(key, part):
    key = jax.random.fold_in(key, 12)
    projection = jnp.clip(jax.random.normal(jax.random.fold_in(key, 1), (DC, 3, DC), jnp.float32), -6.0, 6.0) * DC ** (-0.5)
    return projection.astype(jnp.bfloat16)


def shard_levels(key, extent, shards, low, high):
    def one(dim, shards_of):
        draws = jax.random.uniform(jax.random.fold_in(jax.random.fold_in(key, 6), dim), (shards_of,), jnp.float32, low / len(shards), high / len(shards))
        return jnp.repeat(jnp.exp(draws), extent[dim] // shards_of).reshape((-1,) + (1,) * (len(extent) - dim - 1))

    factor_of = one(*shards[0])
    for cut in shards[1:]:
        factor_of = factor_of * one(*cut)
    return factor_of


def gaussian(stream_key, shape, deviation, limit, shards=(), held_as=jnp.bfloat16):
    array = deviation * jax.random.normal(stream_key, shape, jnp.float32)
    if shards:
        array = array * shard_levels(stream_key, shape, shards, -0.22, 0.18)
    return jnp.clip(array, -limit, limit).astype(held_as)


def setup_inputs(seed: int = 0) -> dict:
    seeds = jax.random.split(jax.random.key(seed), 10)
    return {
        "frames_in": gaussian(seeds[0], (CLIP_FRAME_COUNT, ROWS, COLS, D), 1.0, 6.0, ((0, 64),)),
        "fine_gain": jnp.clip(1.0 + 0.18 * jax.random.normal(seeds[1], (D,), jnp.float32), 0.1, 1.9),
        "fine_query_key_value": draw_fine_query_key_value(jax.random.fold_in(seeds[9], 71), 0),
        "fine_out": gaussian(seeds[3], (D, D), (max(D // 32, 1)) ** -0.5, 1.25, ((0, 4),)),
        "merge_weight": gaussian(seeds[4], (D, DC), (max(D // 16, 1)) ** -0.5, 0.875),
        "coarse_gain": jnp.clip(1.0 + 0.18 * jax.random.normal(seeds[5], (DC,), jnp.float32), 0.1, 1.9),
        "coarse_query_key_value": draw_coarse_query_key_value(jax.random.fold_in(seeds[9], 71), 0),
        "coarse_out": gaussian(seeds[7], (DC, DC), 2.0, 12.0, ((0, 4),)),
        "split_weight": gaussian(seeds[8], (DC, D), DC ** -0.5, 0.15625, ((1, 4),)),
    }


epsilon = 1e-06
reach_space = 3

def stored(value_rows):
    return lax.optimization_barrier(value_rows.astype(jnp.bfloat16))

def rms_scale(value_rows, gain):
    value_rows = value_rows.astype(jnp.float32)
    square_mean = lax.optimization_barrier(jnp.mean(value_rows * value_rows, axis=-1, keepdims=True))
    return value_rows * lax.rsqrt(square_mean + epsilon) * gain.astype(jnp.float32)

def reference(frames_in, fine_gain, fine_query_key_value, fine_out, merge_weight, coarse_gain, coarse_query_key_value, coarse_out, split_weight):
    frame_number, row_count, col_count, feature_count = frames_in.shape
    head_width = feature_count // HEADS
    normalized_input = stored(rms_scale(frames_in, fine_gain))
    qkv_matrix = fine_query_key_value.reshape(feature_count, 3 * feature_count)

    def project(frame_rows):
        flat_rows = frame_rows.reshape(row_count * col_count, feature_count)
        product = jnp.dot(flat_rows, qkv_matrix, preferred_element_type=jnp.float32)
        return stored(product).reshape(row_count, col_count, 3, HEADS, head_width)
    projected = lax.map(project, normalized_input)
    key_values = jnp.pad(projected[:, :, :, 1:], ((1, 1), (0, 0), (0, 0), (0, 0), (0, 0), (0, 0)))
    padded_rows = row_count + 2 * reach_space
    query_index = jnp.arange(row_count * col_count, dtype=jnp.int32)
    query_row = query_index // col_count
    query_col = query_index % col_count
    key_index = jnp.arange(3 * padded_rows * col_count, dtype=jnp.int32)
    key_frame = key_index // (padded_rows * col_count)
    key_row = key_index // col_count % padded_rows - reach_space
    key_col = key_index % col_count
    nearby = (jnp.abs(key_row[None, :] - query_row[:, None]) <= reach_space) & (jnp.abs(key_col[None, :] - query_col[:, None]) <= reach_space)
    nearby = nearby & ((key_row >= 0) & (key_row < row_count))[None, :]

    def attend_frame(frame_at):
        queries = projected[frame_at, :, :, 0].reshape(row_count * col_count, HEADS, head_width)
        slab = lax.dynamic_slice_in_dim(key_values, frame_at, 3, 0)
        slab = jnp.pad(slab, ((0, 0), (reach_space, reach_space), (0, 0), (0, 0), (0, 0), (0, 0)))
        key_block = slab.reshape(3 * padded_rows * col_count, 2, HEADS, head_width)
        source_frame = frame_at + key_frame - 1
        allowed = nearby & ((source_frame >= 0) & (source_frame < frame_number))[None, :]
        scores = jnp.einsum('qhe,khe->hqk', queries.astype(jnp.float32), key_block[:, 0].astype(jnp.float32)) * head_width ** (-0.5)
        masked = jnp.where(allowed[None], scores, -jnp.inf)
        row_max = lax.optimization_barrier(jnp.max(masked, axis=-1, keepdims=True))
        weights = jnp.where(allowed[None], jnp.exp(masked - row_max), 0.0)
        row_total = lax.optimization_barrier(jnp.sum(weights, axis=-1))
        rounded = stored(weights).astype(jnp.float32)
        summed = jnp.einsum('hqk,khe->qhe', rounded, key_block[:, 1].astype(jnp.float32))
        return stored(summed / jnp.transpose(row_total)[:, :, None]).reshape(row_count, col_count, feature_count)
    attended = lax.map(attend_frame, jnp.arange(frame_number, dtype=jnp.int32))

    def out_project(frame_rows):
        return jnp.dot(frame_rows.reshape(row_count * col_count, feature_count), fine_out, preferred_element_type=jnp.float32)
    mixed_heads = lax.map(out_project, attended)
    hidden = stored(frames_in.astype(jnp.float32) + mixed_heads.reshape(frames_in.shape))
    blocks = hidden.astype(jnp.float32).reshape(frame_number // 4, 4, row_count // 4, 4, col_count // 4, 4, feature_count)
    pooled = stored(lax.optimization_barrier(jnp.mean(blocks, axis=(1, 3, 5))))
    coarse = stored(jnp.dot(pooled.reshape(-1, feature_count), merge_weight, preferred_element_type=jnp.float32))
    coarse_width = coarse.shape[1]
    coarse_head = coarse_width // HEADS
    coarse_rms_output = stored(rms_scale(coarse, coarse_gain))
    coarse_proj = stored(jnp.dot(coarse_rms_output, coarse_query_key_value.reshape(coarse_width, 3 * coarse_width), preferred_element_type=jnp.float32))
    coarse_proj = jnp.transpose(coarse_proj.reshape(-1, 3, HEADS, coarse_head), (1, 2, 0, 3))

    def coarse_attend(head_parts):
        queries, keys_here, values_here = head_parts
        scores = jnp.dot(queries, keys_here.T, preferred_element_type=jnp.float32) * coarse_head ** (-0.5)
        row_max = lax.optimization_barrier(jnp.max(scores, axis=-1, keepdims=True))
        weights = jnp.exp(scores - row_max)
        row_total = lax.optimization_barrier(jnp.sum(weights, axis=-1, keepdims=True))
        summed = jnp.dot(stored(weights), values_here, preferred_element_type=jnp.float32)
        return stored(summed / row_total)
    coarse_heads = lax.map(coarse_attend, (coarse_proj[0], coarse_proj[1], coarse_proj[2]))
    coarse_attended = jnp.transpose(coarse_heads, (1, 0, 2)).reshape(-1, coarse_width)
    coarse_after = stored(coarse.astype(jnp.float32) + jnp.dot(coarse_attended, coarse_out, preferred_element_type=jnp.float32))
    split_rows = jnp.dot(coarse_after, split_weight, preferred_element_type=jnp.float32)
    split_grid = split_rows.reshape(frame_number // 4, 1, row_count // 4, 1, col_count // 4, 1, feature_count)
    result = hidden.astype(jnp.float32).reshape(blocks.shape) + split_grid
    return result.reshape(frames_in.shape).astype(jnp.bfloat16)
```

```python
import functools

import jax
import jax.numpy as jnp
import numpy as np
from jax import lax
from jax.experimental import pallas as pl
from jax.experimental.pallas import tpu as pltpu
from jax.sharding import PartitionSpec as P

HEADS = 12
EPSILON = 1e-06
REACH = 3
LOG2E = 1.4426950408889634
ROWS, COLS = 16, 32
TOKENS = ROWS * COLS
FRAMES = ("x", "z", "core")
MIB = 1 << 20
bf16, f32 = jnp.bfloat16, jnp.float32


def nt_dot(a, b):
    return lax.dot_general(a, b, (((1,), (1,)), ((), ())), preferred_element_type=f32)


def nn_dot(a, b):
    return jnp.dot(a, b, preferred_element_type=f32)


def block_mean_matrix():
    token = lax.broadcasted_iota(jnp.int32, (32, TOKENS), 1)
    block = lax.broadcasted_iota(jnp.int32, (32, TOKENS), 0)
    of_token = (token >> 7) * 8 + ((token & 31) >> 2)
    return jnp.where(of_token == block, 1.0 / 64, 0.0).astype(bf16)


def params(mib):
    return pltpu.CompilerParams(vmem_limit_bytes=mib * MIB)


def cost(flops, bytes_accessed, transcendentals=0):
    return pl.CostEstimate(
        flops=int(flops), bytes_accessed=int(bytes_accessed), transcendentals=int(transcendentals)
    )


def key_lanes(head):
    return 128 * head + (0 if head == 1 else 64)


def value_lanes(head):
    return 128 * head + (64 if head == 1 else 0)


def fine_project_kernel(
    x_ref, gain_ref, weight_ref,
    q_ref, key_ref, ones_ref, initial_ref, last_ref, mean_ref, rows_ref,
):
    step = pl.program_id(0)

    @pl.when(step == 0)
    def _():
        for head in range(3):
            k, v, own = key_lanes(head), value_lanes(head), slice(64 * head, 64 * head + 64)
            rows_ref[128 * head : 128 * head + 64, :] = weight_ref[0, own, :]
            rows_ref[128 * head + 64 : 128 * head + 128, :] = jnp.zeros((64, 768), bf16)
            rows_ref[384 + k : 448 + k, :] = weight_ref[1, own, :]
            rows_ref[384 + v : 448 + v, :] = weight_ref[2, own, :]
        mean_ref[...] = jnp.zeros_like(mean_ref)

    x = x_ref[0]
    wide = x.astype(f32)
    scale = lax.rsqrt(jnp.mean(wide * wide, axis=-1, keepdims=True) + EPSILON)
    normed = (wide * scale * gain_ref[...].reshape(1, 768)).astype(bf16)
    projected = nt_dot(normed, rows_ref[...])
    q_ref[0] = (projected[:, :384] * (0.125 * LOG2E)).astype(bf16)
    pairs = projected[:, 384:].astype(bf16)
    keep, fill = value_lane_masks()
    ones_ref[0] = pairs * keep.astype(bf16) + fill.astype(bf16)
    key_ref[0] = nt_dot(weight_ref[1], normed).astype(bf16)
    mean_ref[...] += nn_dot(block_mean_matrix(), x)

    @pl.when(step == 0)
    def _():
        initial_ref[...] = pairs

    @pl.when(step == 3)
    def _():
        last_ref[...] = pairs


def value_lane_masks():
    lane = lax.broadcasted_iota(jnp.int32, (1, 384), 1) >> 6
    is_value = (lane == 0) | (lane == 3) | (lane == 4)
    return jnp.where(is_value, 1.0, 0.0), jnp.where(is_value, 0.0, 1.0)


def in_hbm(*arrays):
    return [pltpu.with_memory_space_constraint(array, pltpu.HBM) for array in arrays]


def fine_project(x, gain, weight):
    x, weight = in_hbm(x, weight)
    return pl.pallas_call(
        fine_project_kernel,
        grid=(4,),
        in_specs=[
            pl.BlockSpec((1, TOKENS, 768), lambda i: (i, 0, 0)),
            pl.BlockSpec((768,), lambda i: (0,)),
            pl.BlockSpec((3, 192, 768), lambda i: (0, 0, 0)),
        ],
        out_specs=[
            pl.BlockSpec((1, TOKENS, 384), lambda i: (i, 0, 0)),
            pl.BlockSpec((1, 192, TOKENS), lambda i: (i, 0, 0)),
            pl.BlockSpec((1, TOKENS, 384), lambda i: (i, 0, 0)),
            whole(TOKENS, 384),
            whole(TOKENS, 384),
            whole(32, 768),
        ],
        out_shape=[
            pltpu.HBM((4, TOKENS, 384), bf16),
            jax.ShapeDtypeStruct((4, 192, TOKENS), bf16),
            jax.ShapeDtypeStruct((4, TOKENS, 384), bf16),
            pltpu.HBM((TOKENS, 384), bf16),
            pltpu.HBM((TOKENS, 384), bf16),
            jax.ShapeDtypeStruct((32, 768), f32),
        ],
        scratch_shapes=[pltpu.VMEM((768, 768), bf16)],
        compiler_params=params(20),
        cost_estimate=cost(2 * 2048 * 768 * 960, 8e6),
        name="fine_project",
    )(x, gain, weight)


BASES = (0, 0, 128, 128)
WINDOWS = ((0, 256), (0, 384), (128, 512), (256, 512))


def near_keys(tile, base):
    query = lax.broadcasted_iota(jnp.int32, (128, 384), 0) + 128 * tile
    key = lax.broadcasted_iota(jnp.int32, (128, 384), 1) + base
    rows = jnp.abs((query >> 5) - (key >> 5))
    cols = jnp.abs((query & 31) - (key & 31))
    return (rows <= REACH) & (cols <= REACH)


def near_masks():
    query = np.arange(512).reshape(4, 128, 1)
    key = np.arange(384).reshape(1, 1, 384) + np.array(BASES).reshape(4, 1, 1)
    rows = np.abs(query // COLS - key // COLS)
    cols = np.abs(query % COLS - key % COLS)
    return jnp.asarray((rows <= REACH) & (cols <= REACH), bf16)


def outside_range(total, least):
    low = lax.broadcasted_iota(jnp.int32, (128, 128), 1) < 64
    bad = jnp.where((total < 2.0**60) & (least > 2.0**-60), 0.0, 1.0)
    return jnp.max(jnp.where(low, bad, 0.0)) > 0.0


def rows_at(part, tile):
    start = part * TOKENS + tile * 128
    return pl.ds(start if isinstance(start, int) else pl.multiple_of(start, 128), 128)


def put_rows(out_ref, tile, pair):
    low = lax.broadcasted_iota(jnp.int32, (128, 128), 1) < 64
    thirds, counts = [], []
    for at, sums in enumerate(pair):
        turned = [pltpu.roll(one, 64, axis=1) for one in sums]
        heads = [one / other for one, other in zip(sums, turned)]
        out_ref[0, rows_at(at, tile), :] = jnp.where(
            low, heads[0], heads[1]
        ).astype(bf16)
        thirds.append(heads[2])
        counts += [turned[0], sums[1], turned[2]]
    packed = jnp.where(low, thirds[0], pltpu.roll(thirds[1], 64, axis=1))
    out_ref[0, rows_at(2, tile), :] = packed.astype(bf16)
    return sum(counts), functools.reduce(jnp.minimum, counts)


def attend_again(q_ref, frames, out_ref):
    def redo(tile, _):
        base = pl.multiple_of((tile >> 1) * 128, 128)
        window, own = pl.ds(base, 384), pl.ds(pl.multiple_of(tile * 128, 128), 128)
        near = near_keys(tile, base)
        pair = []
        for frame, sources in frames:
            sums = []
            for head in range(3):
                query = q_ref[frame, own, 128 * head : 128 * head + 64]
                scores = []
                for keys, _, inside in sources:
                    seen = near if inside is None else near & (inside > 0.0)
                    scored = nn_dot(query, keys[64 * head : 64 * head + 64, window])
                    scores.append(jnp.where(seen, scored, -jnp.inf))
                top = jnp.max(
                    jnp.maximum(jnp.maximum(scores[0], scores[1]), scores[2]),
                    axis=-1,
                    keepdims=True,
                )
                sums.append(
                    sum(
                        nn_dot(
                            jnp.exp2(score - top).astype(bf16),
                            ones[window, 128 * head : 128 * head + 128],
                        )
                        for score, (_, ones, _) in zip(scores, sources)
                    )
                )
            pair.append(sums)
        put_rows(out_ref, tile, pair)
        return 0

    lax.fori_loop(0, 4, redo, 0)


def weigh(query, keys, ones, mask):
    n = query.shape[0]
    weights = jnp.exp2(nn_dot(query.reshape(n * 128, 64), keys)).astype(bf16)
    weights = (weights.reshape(n, *mask.shape) * mask[None]).reshape(n * 128, mask.shape[1])
    return nn_dot(weights, ones).reshape(n, 128, 128)


def tiles():
    for tile in range(4):
        first, last = WINDOWS[tile]
        own = slice(128 * tile, 128 * tile + 128)
        yield tile, own, slice(first, last), slice(first - BASES[tile], last - BASES[tile])


def head_slices(head):
    return (
        slice(128 * head, 128 * head + 64),
        slice(64 * head, 64 * head + 64),
        slice(128 * head, 128 * head + 128),
    )


def block_means(out_ref):
    matrix = block_mean_matrix()
    pairs = nn_dot(matrix, out_ref[0, :TOKENS, :])
    pairs += nn_dot(matrix, out_ref[0, TOKENS : 2 * TOKENS, :])
    return pairs, nn_dot(matrix, out_ref[0, 2 * TOKENS :, :])


def inner_kernel(mask_ref, q_ref, k_ref, v_ref, out_ref, mean_ref, part_ref):
    total, least = jnp.zeros((128, 128), f32), jnp.ones((128, 128), f32)
    for tile, own, window, seen in tiles():
        pair = [[], []]
        for head in range(3):
            q_lanes, k_rows, lanes = head_slices(head)
            sums = [None] * 4
            for g in range(4):
                lo, hi = max(g - 1, 0), min(g + 1, 3)
                parts = weigh(
                    q_ref[lo : hi + 1, own, q_lanes],
                    k_ref[g, k_rows, window],
                    v_ref[g, window, lanes],
                    mask_ref[tile, :, seen],
                )
                for f in range(lo, hi + 1):
                    sums[f] = parts[f - lo] if sums[f] is None else sums[f] + parts[f - lo]
            part_ref[0, own, lanes] = sums[0]
            part_ref[1, own, lanes] = sums[3]
            pair[0].append(sums[1])
            pair[1].append(sums[2])
        tile_total, tile_least = put_rows(out_ref, tile, pair)
        total, least = total + tile_total, jnp.minimum(least, tile_least)

    @pl.when(outside_range(total, least))
    def _():
        own_frames = [(k_ref.at[g], v_ref.at[g], None) for g in range(4)]
        attend_again(q_ref, [(1, own_frames[:3]), (2, own_frames[1:])], out_ref)

    mean_ref[:, :128], mean_ref[:, 128:] = block_means(out_ref)


def outer_kernel(
    edge_ref, mask_ref, q_ref, k_ref, v_ref, part_ref, first_ref, last_ref, inner_mean_ref,
    weight_ref, inner_ref, out_ref, partial_ref, halo_key_ref, halo_ones_ref,
):
    keep, fill = value_lane_masks()
    for at, halo_ref in enumerate((first_ref, last_ref)):
        halo, inside = halo_ref[...].astype(f32), edge_ref[at]
        halo_ones_ref[at] = (halo * (keep * inside) + fill * inside).astype(bf16)
        turned = jnp.transpose(halo).astype(bf16)
        for head in range(3):
            start = key_lanes(head)
            halo_key_ref[at, 64 * head : 64 * head + 64, :] = turned[start : start + 64]

    total, least = jnp.zeros((128, 128), f32), jnp.ones((128, 128), f32)
    for tile, own, window, seen in tiles():
        pair = [[], []]
        for head in range(3):
            q_lanes, k_rows, lanes = head_slices(head)
            for at, frame in enumerate((0, 3)):
                more = weigh(
                    q_ref[frame : frame + 1, own, q_lanes],
                    halo_key_ref[at, k_rows, window],
                    halo_ones_ref[at, window, lanes],
                    mask_ref[tile, :, seen],
                )
                pair[at].append(part_ref[at, own, lanes] + more[0])
        tile_total, tile_least = put_rows(out_ref, tile, pair)
        total, least = total + tile_total, jnp.minimum(least, tile_least)

    @pl.when(outside_range(total, least))
    def _():
        own_frames = [(k_ref.at[g], v_ref.at[g], None) for g in range(4)]
        halos = [(halo_key_ref.at[at], halo_ones_ref.at[at], edge_ref[at]) for at in (0, 1)]
        attend_again(
            q_ref, [(0, own_frames[:2] + halos[:1]), (3, own_frames[2:] + halos[1:])], out_ref
        )

    here = block_means(out_ref)
    pairs = here[0] + inner_mean_ref[:, :128]
    third = here[1] + inner_mean_ref[:, 128:]
    third = third + pltpu.roll(third, 64, axis=1)
    partial = nn_dot(pairs.astype(bf16), weight_ref[:128, :])
    partial += nn_dot(third[:, :64].astype(bf16), weight_ref[128:, :])
    partial_ref[...] = partial.astype(bf16)


def whole(*shape):
    return pl.BlockSpec(shape, lambda *i: (0,) * len(shape))


def attend_inner(mask, q, k, v):
    return pl.pallas_call(
        inner_kernel,
        grid=(1,),
        in_specs=[pl.BlockSpec(memory_space=pltpu.VMEM)] * 4,
        out_specs=[
            pl.BlockSpec((1, 3 * TOKENS, 128), lambda i: (0, 0, 0)),
            whole(32, 256),
            whole(2, TOKENS, 384),
        ],
        out_shape=[
            pltpu.HBM((2, 3 * TOKENS, 128), bf16),
            jax.ShapeDtypeStruct((32, 256), f32),
            jax.ShapeDtypeStruct((2, TOKENS, 384), f32),
        ],
        compiler_params=params(24),
        cost_estimate=cost(10 * 2 * 512 * 320 * 3 * 256, 6e6, 10 * 512 * 320 * 3),
        name="attend_inner",
    )(mask, q, k, v)


def attend_outer(edge, mask, q, k, v, part, first, last, inner_mean, weight, inner):
    vmem = pl.BlockSpec(memory_space=pltpu.VMEM)
    return pl.pallas_call(
        outer_kernel,
        grid=(1,),
        in_specs=[pl.BlockSpec(memory_space=pltpu.SMEM)]
        + [vmem] * 9
        + [pl.BlockSpec(memory_space=pltpu.HBM)],
        out_specs=[pl.BlockSpec((1, 3 * TOKENS, 128), lambda i: (1, 0, 0)), whole(32, 768)],
        out_shape=[
            pltpu.HBM((2, 3 * TOKENS, 128), bf16),
            jax.ShapeDtypeStruct((32, 768), bf16),
        ],
        input_output_aliases={10: 0},
        scratch_shapes=[
            pltpu.VMEM((2, 192, TOKENS), bf16),
            pltpu.VMEM((2, TOKENS, 384), bf16),
        ],
        compiler_params=params(24),
        cost_estimate=cost(2 * 2 * 512 * 320 * 3 * 256, 6e6, 2 * 512 * 320 * 3),
        name="attend_outer",
    )(edge, mask, q, k, v, part, first, last, inner_mean, weight, inner)


def load_kernel(_, merge_ref, weight_ref, merge_out, weight_out, sems):
    copies = [
        pltpu.make_async_copy(merge_ref, merge_out, sems.at[0]),
        pltpu.make_async_copy(weight_ref, weight_out, sems.at[1]),
    ]
    for copy in copies:
        copy.start()
    for copy in copies:
        copy.wait()


def load_weights(after, merge, weight):
    anywhere = pl.BlockSpec(memory_space=pl.ANY)
    return pl.pallas_call(
        load_kernel,
        in_specs=[anywhere] * 3,
        out_specs=[anywhere] * 2,
        out_shape=[pltpu.VMEM(merge.shape, bf16), pltpu.VMEM(weight.shape, bf16)],
        scratch_shapes=[pltpu.SemaphoreType.DMA((2,))],
        compiler_params=params(4),
        cost_estimate=cost(0, 6e6),
        name="load_weights",
    )(after, *in_hbm(merge, weight))


def coarse_project_kernel(
    p0, p1, p2, p3, mean_ref, merge_ref, gain_ref, weight_ref, coarse_ref, q_ref, kv_ref
):
    pooled = mean_ref[...] + (
        (p0[...].astype(f32) + p1[...].astype(f32)) + (p2[...].astype(f32) + p3[...].astype(f32))
    )
    coarse = nn_dot(pooled.astype(bf16), merge_ref[...]).astype(bf16)
    coarse_ref[...] = coarse
    wide = coarse.astype(f32)
    scale = lax.rsqrt(jnp.mean(wide * wide, axis=-1, keepdims=True) + EPSILON)
    normed = (wide * scale * gain_ref[...].reshape(1, 1536)).astype(bf16)
    q_ref[...] = (nn_dot(normed, weight_ref[0]) * (128**-0.5 * LOG2E)).astype(bf16)
    key = nn_dot(normed, weight_ref[1]).astype(bf16)
    value = nn_dot(normed, weight_ref[2]).astype(bf16)
    for copy in range(8):
        kv_ref[copy, :, :384] = key
        kv_ref[copy, :, 384:] = value


def coarse_project(partials, mean, merge, gain, weight):
    return pl.pallas_call(
        coarse_project_kernel,
        in_specs=[pl.BlockSpec(memory_space=pltpu.VMEM)] * 8,
        out_specs=[whole(32, 1536), whole(32, 384), whole(8, 32, 768)],
        out_shape=[
            jax.ShapeDtypeStruct((32, 1536), bf16),
            jax.ShapeDtypeStruct((32, 384), bf16),
            pltpu.HBM((8, 32, 768), bf16),
        ],
        compiler_params=params(20),
        cost_estimate=cost(2 * 32 * 1536 * 1920, 7e6),
        name="coarse_project",
    )(*partials, mean, merge, gain, weight)


def coarse_attend_kernel(q0, q1, q2, q3, kv_ref, other_ref, o0, o1, o2, o3):
    query = jnp.concatenate([ref[...] for ref in (q0, q1, q2, q3)], axis=0)
    outs = (o0, o1, o2, o3)
    lane = lax.broadcasted_iota(jnp.int32, (128, 128), 1)
    stats = jnp.zeros((128, 128), f32)
    for head in range(3):
        lanes = slice(128 * head, 128 * head + 128)
        values = slice(384 + 128 * head, 512 + 128 * head)
        scores = [nt_dot(query[:, lanes], ref[:, lanes]) for ref in (kv_ref, other_ref)]
        top = jnp.max(jnp.maximum(scores[0], scores[1]), axis=-1, keepdims=True)
        weights = [jnp.exp2(score - top) for score in scores]
        total = jnp.sum(weights[0] + weights[1], axis=-1, keepdims=True)
        summed = nn_dot(weights[0].astype(bf16), kv_ref[:, values])
        summed += nn_dot(weights[1].astype(bf16), other_ref[:, values])
        summed = (summed / total).astype(bf16)
        rest = top + jnp.log(total) * LOG2E
        for part in range(3):
            piece = rest.astype(bf16).astype(f32)
            stats = jnp.where(lane == 3 * head + part, piece, stats)
            rest = rest - piece
        for i, out in enumerate(outs):
            out[:, lanes] = summed[32 * i : 32 * i + 32]
    for i, out in enumerate(outs):
        out[:, 384:] = stats[32 * i : 32 * i + 32].astype(bf16)


def coarse_attend(queries, kv, other):
    return pl.pallas_call(
        coarse_attend_kernel,
        out_shape=[jax.ShapeDtypeStruct((32, 512), bf16)] * 4,
        compiler_params=params(16),
        cost_estimate=cost(4 * 128 * 512 * 384, 1e6, 128 * 512 * 3),
        name="coarse_attend",
    )(*queries, kv, other)


def coarse_combine_kernel(p0, p1, p2, p3, weight_ref, out_ref):
    parts = (p0, p1, p2, p3)
    heads = []
    for head in range(3):
        lanes = slice(128 * head, 128 * head + 128)
        logs = [
            jnp.sum(part[:, 384 + 3 * head : 387 + 3 * head].astype(f32), axis=-1, keepdims=True)
            for part in parts
        ]
        top = functools.reduce(jnp.maximum, logs)
        shares = [jnp.exp2(log - top) for log in logs]
        summed = sum(share * part[:, lanes].astype(f32) for share, part in zip(shares, parts))
        heads.append((summed / sum(shares)).astype(bf16))
    attended = jnp.concatenate(heads, axis=-1)
    out_ref[...] = nn_dot(attended, weight_ref[...]).astype(bf16)


def coarse_combine(parts, weight):
    return pl.pallas_call(
        coarse_combine_kernel,
        out_shape=jax.ShapeDtypeStruct((32, 1536), bf16),
        compiler_params=params(16),
        cost_estimate=cost(2 * 32 * 384 * 1536, 2e6),
        name="coarse_combine",
    )(*parts, weight)


def own_features_kernel(place_ref, x_ref, weight_ref, x_out, pair_ref, low_ref, high_ref, pick_ref):
    step = pl.program_id(0)

    @pl.when(step == 0)
    def _():
        place = place_ref[0] * 192
        row = lax.broadcasted_iota(jnp.int32, (768, 192), 0)
        col = lax.broadcasted_iota(jnp.int32, (768, 192), 1)
        pick_ref[...] = jnp.where(row == col + place, 1.0, 0.0).astype(bf16)
        zeros = jnp.zeros((64, 192), bf16)
        for s in range(4):
            weight = nn_dot(weight_ref[s], pick_ref[...]).astype(bf16)
            pair_ref[128 * s : 128 * s + 128, :] = weight[:128]
            low_ref[128 * s : 128 * s + 64, :] = weight[128:]
            low_ref[128 * s + 64 : 128 * s + 128, :] = zeros
            high_ref[128 * s : 128 * s + 64, :] = zeros
            high_ref[128 * s + 64 : 128 * s + 128, :] = weight[128:]

    x_out[0] = nn_dot(x_ref[0], pick_ref[...]).astype(bf16)


def row_place(frame):
    return jnp.where(frame == 3, 3, (frame + 2) % 3)


def own_features(place, x, weight):
    x, weight = in_hbm(x, weight)
    return pl.pallas_call(
        own_features_kernel,
        grid=(4,),
        in_specs=[
            pl.BlockSpec(memory_space=pltpu.SMEM),
            pl.BlockSpec((1, TOKENS, 768), lambda i: (i, 0, 0)),
            whole(4, 192, 768),
        ],
        out_specs=[pl.BlockSpec((1, TOKENS, 192), lambda i: (row_place(i), 0, 0))]
        + [whole(512, 192)] * 3,
        out_shape=[jax.ShapeDtypeStruct((4, TOKENS, 192), bf16)]
        + [jax.ShapeDtypeStruct((512, 192), bf16)] * 3,
        scratch_shapes=[pltpu.VMEM((768, 192), bf16)],
        compiler_params=params(16),
        cost_estimate=cost(2 * 2048 * 192 * 768, 5e6),
        name="own_features",
    )(place, x, weight)


def hidden_kernel(x_ref, rows_ref, pair_ref, low_ref, high_ref, out_ref):
    parts = [
        jnp.concatenate([rows_ref[s, 0, TOKENS * i : TOKENS * (i + 1)] for s in range(4)], axis=1)
        for i in range(3)
    ]
    for at, third_ref in enumerate((low_ref, high_ref)):
        mixed = nn_dot(parts[at], pair_ref[...]) + nn_dot(parts[2], third_ref[...])
        out_ref[at] = (x_ref[at].astype(f32) + mixed).astype(bf16)


def hidden_rows(x, rows, pair, low, high):
    (rows,) = in_hbm(rows)
    return pl.pallas_call(
        hidden_kernel,
        grid=(2,),
        in_specs=[
            pl.BlockSpec((2, TOKENS, 192), lambda i: (i, 0, 0)),
            pl.BlockSpec((4, 1, 3 * TOKENS, 128), lambda i: (0, i, 0, 0)),
        ]
        + [whole(512, 192)] * 3,
        out_specs=pl.BlockSpec((2, TOKENS, 192), lambda i: (i, 0, 0)),
        out_shape=jax.ShapeDtypeStruct((4, TOKENS, 192), bf16),
        compiler_params=params(20),
        cost_estimate=cost(2 * 2048 * 192 * 1024, 5e6),
        name="hidden_rows",
    )(x, rows, pair, low, high)


def split_kernel(hidden_ref, coarse_ref, p0, p1, p2, p3, weight_ref, out_ref):
    mixed = (p0[...].astype(f32) + p1[...].astype(f32)) + (
        p2[...].astype(f32) + p3[...].astype(f32)
    )
    after = (coarse_ref[...].astype(f32) + mixed).astype(bf16)
    split = nt_dot(after, weight_ref[...])
    row = lax.broadcasted_iota(jnp.int32, (128, 32), 0)
    col = lax.broadcasted_iota(jnp.int32, (128, 32), 1)
    spread = jnp.where(col == (row >> 5) * 8 + ((row & 31) >> 2), 1.0, 0.0)
    grid = jnp.dot(spread, split, preferred_element_type=f32, precision=lax.Precision.HIGHEST)
    for at_frame, frame in enumerate((1, 2, 0, 3)):
        for block in range(4):
            rows = grid[32 * block : 32 * block + 32]
            for r in range(4):
                at = 4 * block + r
                here = hidden_ref[at_frame, at * COLS : (at + 1) * COLS, :].astype(f32)
                out_ref[frame, at] = (here + rows).astype(bf16)


def split_rows(hidden, coarse, partials, weight):
    return pl.pallas_call(
        split_kernel,
        out_shape=jax.ShapeDtypeStruct((4, ROWS, COLS, 192), bf16),
        compiler_params=params(20),
        cost_estimate=cost(2 * 32 * 1536 * 192, 4e6),
        name="split_rows",
    )(hidden, coarse, *partials, weight)


def shifted(value, axis, shift):
    return lax.ppermute(value, axis, [(i, (i + shift) % 4) for i in range(4)])


def from_others(value, axis):
    return [shifted(value, axis, shift) for shift in (1, 2, 3)]


def body(x, fine_gain, fine_qkv, fine_out, merge, coarse_gain, coarse_qkv, coarse_out, split):
    x = x.reshape(4, TOKENS, 768)
    groups = lax.axis_size(FRAMES)
    here = lax.axis_index(FRAMES)
    place = lax.axis_index("mp").astype(jnp.int32).reshape(1)
    edge = jnp.stack(
        [jnp.where(here == 0, 0.0, 1.0), jnp.where(here == groups - 1, 0.0, 1.0)]
    ).astype(f32)

    fine_outs = lax.all_gather(fine_out, "mp", axis=0)
    q, k, v, initial, final, frame_mean = fine_project(
        x, fine_gain, jnp.transpose(fine_qkv, (1, 2, 0))
    )
    first = lax.ppermute(final, FRAMES, [(i, i + 1) for i in range(groups - 1)])
    last = lax.ppermute(initial, FRAMES, [(i + 1, i) for i in range(groups - 1)])
    mask = near_masks()
    inner, inner_mean, part = attend_inner(mask, q, k, v)
    rows, partial = attend_outer(
        edge, mask, q, k, v, part, first, last, inner_mean, fine_out, inner
    )
    partials = [partial] + from_others(partial, "mp")
    merge, coarse_qkv = load_weights(partials[1], merge, jnp.transpose(coarse_qkv, (1, 0, 2)))
    rows = lax.all_gather(rows, "mp", axis=0)

    coarse, coarse_q, coarse_kv = coarse_project(
        partials, frame_mean, merge, coarse_gain, coarse_qkv
    )
    coarse_kv = lax.all_to_all(coarse_kv, "z", 0, 0, tiled=True).reshape(256, 768)
    queries = [coarse_q] + from_others(coarse_q, "x")
    own = own_features(place, x, fine_outs)
    coarse_kv, queries, own = lax.optimization_barrier((coarse_kv, queries, own))
    other_kv = lax.ppermute(coarse_kv, "core", [(0, 1), (1, 0)])
    parts = list(coarse_attend(queries, coarse_kv, other_kv))
    parts = parts[:1] + [shifted(parts[s], "x", 4 - s) for s in (1, 2, 3)]
    coarse_partial = coarse_combine(parts, coarse_out)
    coarse_partials = [coarse_partial] + from_others(coarse_partial, "mp")
    hidden = hidden_rows(own[0], rows, *own[1:])
    return split_rows(hidden, coarse, coarse_partials, jnp.transpose(split, (1, 0)))


def solution(mesh):
    parts = jax.sharding.Mesh(mesh.devices.reshape(4, 8, 2, 4), FRAMES + ("mp",))
    in_specs = (
        P(FRAMES, None, None, None),
        P(),
        P(None, None, "mp"),
        P("mp", None),
        P(),
        P(),
        P(None, None, "mp"),
        P("mp", None),
        P(None, "mp"),
    )
    out_specs = P(FRAMES, None, None, "mp")
    return jax.shard_map(body, mesh=parts, in_specs=in_specs, out_specs=out_specs, check_vma=False)
```

```python
import functools

import jax
import jax.numpy as jnp
from jax import lax
from jax.experimental import pallas as pl
from jax.experimental.pallas import tpu as pltpu
from jax.sharding import PartitionSpec as P

HEADS = 12
EPSILON = 1e-06
REACH = 3
LOG2E = 1.4426950408889634
ROWS, COLS = 16, 32
TOKENS = ROWS * COLS
FRAMES = ("x", "z", "core")
MIB = 1 << 20
bf16, f32 = jnp.bfloat16, jnp.float32


def nt_dot(a, b):
    return lax.dot_general(a, b, (((1,), (1,)), ((), ())), preferred_element_type=f32)


def nn_dot(a, b):
    return jnp.dot(a, b, preferred_element_type=f32)


def block_mean_matrix(rows):
    token = lax.broadcasted_iota(jnp.int32, (32, rows * COLS), 1)
    block = lax.broadcasted_iota(jnp.int32, (32, rows * COLS), 0)
    of_token = token // (rows * COLS // 4) * 8 + ((token & 31) >> 2)
    return jnp.where(of_token == block, 1.0 / 64, 0.0)


def params(mib):
    return pltpu.CompilerParams(vmem_limit_bytes=mib * MIB)


def cost(flops, bytes_accessed, transcendentals=0):
    return pl.CostEstimate(
        flops=int(flops), bytes_accessed=int(bytes_accessed), transcendentals=int(transcendentals)
    )


def whole(*shape):
    return pl.BlockSpec(shape, lambda *i: (0,) * len(shape))


def fine_project_kernel(
    place_ref, x_hbm, gain_hbm, weight_hbm,
    q_ref, key_ref, ones_ref, initial_hbm, last_hbm, mean_hbm, own_hbm,
    x_ref, gain_ref, weight_ref, rows_ref, sum_ref, edge_ref, own_ref, mean_ref,
    in_sems, out_sems,
):
    gain_copy = pltpu.make_async_copy(gain_hbm, gain_ref, in_sems.at[5])
    gain_copy.start()
    weight_copy = pltpu.make_async_copy(weight_hbm, weight_ref, in_sems.at[4])
    weight_copy.start()
    x_copies = [
        pltpu.make_async_copy(x_hbm.at[frame], x_ref.at[frame], in_sems.at[frame])
        for frame in range(4)
    ]
    order = (0, 3, 1, 2)
    for frame in order:
        x_copies[frame].start()
    gain_copy.wait()
    weight_copy.wait()
    gain = gain_ref[...].reshape(1, 768)
    query, key, value = (weight_ref[i].astype(f32) * gain for i in range(3))
    rows_ref[:192, :] = value.astype(bf16)
    rows_ref[192:384, :] = key.astype(bf16)
    rows_ref[384:, :] = (query * (0.125 * LOG2E)).astype(bf16)

    out_copies = [
        pltpu.make_async_copy(edge_ref.at[i], out, out_sems.at[i])
        for i, out in enumerate((initial_hbm, last_hbm))
    ]

    for step, frame in enumerate(order):
        x_copies[frame].wait()
        if step == 3:
            for place in range(4):

                @pl.when(place_ref[0] == place)
                def _():
                    own_ref[...] = x_ref[:, :, 192 * place : 192 * place + 192]

            out_copies.append(pltpu.make_async_copy(own_ref, own_hbm, out_sems.at[2]))
            out_copies[-1].start()
        x = x_ref[frame]
        wide = x.astype(f32)
        projected = nt_dot(x, rows_ref[...])
        scale = lax.rsqrt(jnp.mean(wide * wide, axis=-1, keepdims=True) + EPSILON)
        projected = projected * scale
        q_ref[frame] = projected[:, 384:].astype(bf16)
        pairs = projected[:, :384]
        lane = lax.broadcasted_iota(jnp.int32, (1, 256), 1)
        ones_ref[frame] = jnp.where(lane < 192, projected[:, :256], 1.0).astype(bf16)
        along = jnp.transpose(jnp.broadcast_to(scale, (TOKENS, 128)))[:1]
        key_ref[frame] = (nt_dot(rows_ref[192:384, :], x) * along).astype(bf16)
        added = jnp.sum(wide.reshape(4, 4, COLS, 768), axis=1).reshape(4 * COLS, 768)
        sum_ref[...] = sum_ref[...] + added if step else added
        if step < 2:
            edge_ref[step] = pairs.astype(bf16)
            out_copies[step].start()
    mean_ref[...] = jnp.dot(
        block_mean_matrix(4),
        sum_ref[...],
        preferred_element_type=f32,
        precision=lax.Precision.HIGHEST,
    )
    out_copies.append(pltpu.make_async_copy(mean_ref, mean_hbm, out_sems.at[3]))
    out_copies[-1].start()
    for copy in out_copies:
        copy.wait()


def in_hbm(*arrays):
    return [pltpu.with_memory_space_constraint(array, pltpu.HBM) for array in arrays]


def fine_project(place, x, gain, weight):
    vmem, hbm = pl.BlockSpec(memory_space=pltpu.VMEM), pl.BlockSpec(memory_space=pltpu.HBM)
    return pl.pallas_call(
        fine_project_kernel,
        in_specs=[pl.BlockSpec(memory_space=pltpu.SMEM), hbm, hbm, hbm],
        out_specs=[vmem, vmem, vmem, hbm, hbm, hbm, hbm],
        out_shape=[
            jax.ShapeDtypeStruct((4, TOKENS, 192), bf16),
            jax.ShapeDtypeStruct((4, 192, TOKENS), bf16),
            jax.ShapeDtypeStruct((4, TOKENS, 256), bf16),
            pltpu.HBM((TOKENS, 384), bf16),
            pltpu.HBM((TOKENS, 384), bf16),
            pltpu.HBM((32, 768), f32),
            pltpu.HBM((4, TOKENS, 192), bf16),
        ],
        scratch_shapes=[
            pltpu.VMEM((4, TOKENS, 768), bf16),
            pltpu.VMEM((768,), f32),
            pltpu.VMEM((3, 192, 768), bf16),
            pltpu.VMEM((576, 768), bf16),
            pltpu.VMEM((128, 768), f32),
            pltpu.VMEM((2, TOKENS, 384), bf16),
            pltpu.VMEM((4, TOKENS, 192), bf16),
            pltpu.VMEM((32, 768), f32),
            pltpu.SemaphoreType.DMA((6,)),
            pltpu.SemaphoreType.DMA((4,)),
        ],
        compiler_params=params(24),
        cost_estimate=cost(2 * 2048 * 768 * 768, 8e6),
        name="fine_project",
    )(place, *in_hbm(x, gain, weight))


BASES = (0, 0, 128, 128)
WINDOWS = ((0, 256), (0, 384), (128, 512), (256, 512))


def near_keys(tile, base):
    query = lax.broadcasted_iota(jnp.int32, (128, 384), 0) + 128 * tile
    key = lax.broadcasted_iota(jnp.int32, (128, 384), 1) + base
    rows = jnp.abs((query >> 5) - (key >> 5))
    cols = jnp.abs((query & 31) - (key & 31))
    return (rows <= REACH) & (cols <= REACH)


def outside_range(total, least):
    low = lax.broadcasted_iota(jnp.int32, (128, 128), 1) < 64
    bad = jnp.where((total < 2.0**60) & (least > 2.0**-60), 0.0, 1.0)
    return jnp.max(jnp.where(low, bad, 0.0))


def rows_at(part, tile):
    start = part * TOKENS + tile * 128
    return pl.ds(start if isinstance(start, int) else pl.multiple_of(start, 128), 128)


def window_of(tile):
    base = pl.multiple_of((tile >> 1) * 128, 128)
    return base, pl.ds(base, 384), pl.ds(pl.multiple_of(tile * 128, 128), 128)


def put_rows(out_ref, tile, pair):
    low = lax.broadcasted_iota(jnp.int32, (128, 128), 1) < 64
    thirds, counts = [], []
    for at, sums in enumerate(pair):
        turned = [pltpu.roll(one, 64, axis=1) for one in sums]
        heads = [one / other for one, other in zip(sums, turned)]
        out_ref[0, rows_at(at, tile), :] = jnp.where(
            low, heads[0], heads[1]
        ).astype(bf16)
        thirds.append(heads[2])
        counts += [turned[0], sums[1], turned[2]]
    packed = jnp.where(low, thirds[0], pltpu.roll(thirds[1], 64, axis=1))
    out_ref[0, rows_at(2, tile), :] = packed.astype(bf16)
    return sum(counts), functools.reduce(jnp.minimum, counts)


def stack_heads(query):
    head = lax.broadcasted_iota(jnp.int32, (1, 192), 1) >> 6
    return jnp.concatenate(
        [query * jnp.where(head == i, 1.0, 0.0).astype(bf16) for i in range(3)], axis=0
    )


def own_parts(summed):
    low = lax.broadcasted_iota(jnp.int32, (1, 128, 128), 2) < 64
    first, second = summed[..., :128], summed[..., 128:]
    n = summed.shape[1]
    turned = pltpu.roll(second[1].reshape(n * 128, 128), 64, axis=1).reshape(n, 128, 128)
    return [
        jnp.where(low, first[0], second[0]),
        jnp.where(low, turned, first[1]),
        second[2],
    ]


def attend_again(q_ref, frames, out_ref):
    def redo(tile, _):
        base, window, own = window_of(tile)
        near = jnp.concatenate([near_keys(tile, base)] * 3, axis=0)
        pair = []
        for frame, sources in frames:
            query = stack_heads(q_ref[frame, own, :])
            scores = []
            for keys, _, inside in sources:
                seen = near if inside is None else near & (inside > 0.0)
                scores.append(jnp.where(seen, nn_dot(query, keys[:, window]), -jnp.inf))
            top = jnp.max(
                jnp.maximum(jnp.maximum(scores[0], scores[1]), scores[2]), axis=-1, keepdims=True
            )
            summed = sum(
                nn_dot(jnp.exp2(score - top).astype(bf16), ones[window, :])
                for score, (_, ones, _) in zip(scores, sources)
            )
            pair.append([part[0] for part in own_parts(summed.reshape(3, 1, 128, 256))])
        put_rows(out_ref, tile, pair)
        return 0

    lax.fori_loop(0, 4, redo, 0)


def weigh(query, keys, ones, mask):
    n = query.shape[0]
    weights = jnp.exp2(nn_dot(stack_heads(query.reshape(n * 128, 192)), keys)).astype(bf16)
    weights = (weights.reshape(3 * n, *mask.shape) * mask[None]).reshape(-1, mask.shape[1])
    return own_parts(nn_dot(weights, ones).reshape(3, n, 128, 256))


def tiles():
    for tile in range(4):
        first, last = WINDOWS[tile]
        own = slice(128 * tile, 128 * tile + 128)
        yield tile, own, slice(first, last), slice(first - BASES[tile], last - BASES[tile])


def block_means(out_ref):
    matrix = block_mean_matrix(ROWS).astype(bf16)
    pairs = nn_dot(matrix, out_ref[0, :TOKENS, :])
    pairs += nn_dot(matrix, out_ref[0, TOKENS : 2 * TOKENS, :])
    return pairs, nn_dot(matrix, out_ref[0, 2 * TOKENS :, :])


def set_weights(weight_ref, first_ref, third_ref):
    first_ref[...] = jnp.zeros_like(first_ref)
    third_ref[...] = jnp.zeros_like(third_ref)
    for place in range(4):
        weight = weight_ref[:, 192 * place : 192 * place + 192]
        lanes = slice(128 * place, 128 * place + 128)
        for at in (0, 1):
            first_ref[at, :128, lanes] = weight[:128, :128]
            first_ref[at, 128 + 64 * at : 192 + 64 * at, lanes] = weight[128:, :128]
            half = slice(128 * place + 64 * at, 128 * place + 64 * at + 64)
            third_ref[128 * at : 128 * at + 128, half] = weight[:128, 128:]
            third_ref[256 + 64 * at : 320 + 64 * at, half] = weight[128:, 128:]


def put_products(rows_ref, first_ref, third_ref, out_ref, out_hbm, sems):
    parts = [rows_ref[0, TOKENS * i : TOKENS * (i + 1), :] for i in range(3)]
    copies = []
    for i in range(3):
        if i < 2:
            product = nn_dot(jnp.concatenate([parts[i], parts[2]], axis=1), first_ref[i])
        else:
            product = nn_dot(jnp.concatenate(parts, axis=1), third_ref[...])
        own = pl.ds(TOKENS * i, TOKENS)
        for place in range(4):
            out_ref[place, own, :] = product[:, 128 * place : 128 * place + 128].astype(bf16)
        copies.append(
            pltpu.make_async_copy(out_ref.at[:, own, :], out_hbm.at[:, own, :], sems.at[i])
        )
        copies[-1].start()
    for copy in copies:
        copy.wait()


def inner_kernel(
    q_ref, k_ref, v_ref, weight_hbm,
    out_hbm, mask_ref, mean_ref, part_ref, first_ref, third_ref, rows_ref, out_ref, weight_ref, sems,
):
    weight_copy = pltpu.make_async_copy(weight_hbm, weight_ref, sems.at[3])
    weight_copy.start()

    total, least = jnp.zeros((128, 128), f32), jnp.ones((128, 128), f32)
    for tile, own, window, seen in tiles():
        mask_ref[tile] = jnp.where(near_keys(tile, BASES[tile]), 1.0, 0.0).astype(bf16)
        sums = [None] * 4
        for g in range(4):
            lo, hi = max(g - 1, 0), min(g + 1, 3)
            parts = weigh(
                q_ref[lo : hi + 1, own, :],
                k_ref[g, :, window],
                v_ref[g, window, :],
                mask_ref[tile, :, seen],
            )
            for f in range(lo, hi + 1):
                here = [part[f - lo] for part in parts]
                sums[f] = here if sums[f] is None else [a + b for a, b in zip(sums[f], here)]
        for head in range(3):
            lanes = slice(128 * head, 128 * head + 128)
            part_ref[0, own, lanes] = sums[0][head]
            part_ref[1, own, lanes] = sums[3][head]
        tile_total, tile_least = put_rows(rows_ref, tile, sums[1:3])
        total, least = total + tile_total, jnp.minimum(least, tile_least)
    bad = outside_range(total, least)

    @pl.when(bad > 0.0)
    def _():
        own_frames = [(k_ref.at[g], v_ref.at[g], None) for g in range(4)]
        attend_again(q_ref, [(1, own_frames[:3]), (2, own_frames[1:])], rows_ref)

    mean_ref[:, :128], mean_ref[:, 128:] = block_means(rows_ref)
    weight_copy.wait()
    set_weights(weight_ref, first_ref, third_ref)
    put_products(rows_ref, first_ref, third_ref, out_ref, out_hbm.at[:, 0], sems)


def outer_kernel(
    edge_ref, mask_ref, q_ref, k_ref, v_ref, part_ref, halo_first_ref, halo_last_ref,
    inner_mean_ref, first_ref, third_ref, weight_hbm, inner_ref,
    out_hbm, partial_ref, halo_key_ref, halo_ones_ref,
    rows_ref, out_ref, weight_ref, sems,
):
    weight_copy = pltpu.make_async_copy(weight_hbm, weight_ref, sems.at[3])
    weight_copy.start()
    lane = lax.broadcasted_iota(jnp.int32, (1, 256), 1)
    for at, halo_ref in enumerate((halo_first_ref, halo_last_ref)):
        halo = halo_ref[...].astype(f32)
        halo_ones_ref[at] = (jnp.where(lane < 192, halo[:, :256], 1.0) * edge_ref[at]).astype(bf16)
        halo_key_ref[at] = jnp.transpose(halo)[192:].astype(bf16)

    total, least = jnp.zeros((128, 128), f32), jnp.ones((128, 128), f32)
    for tile, own, window, seen in tiles():
        pair = []
        for at, frame in enumerate((0, 3)):
            more = weigh(
                q_ref[frame : frame + 1, own, :],
                halo_key_ref[at, :, window],
                halo_ones_ref[at, window, :],
                mask_ref[tile, :, seen],
            )
            pair.append(
                [
                    part_ref[at, own, 128 * head : 128 * head + 128] + more[head][0]
                    for head in range(3)
                ]
            )
        tile_total, tile_least = put_rows(rows_ref, tile, pair)
        total, least = total + tile_total, jnp.minimum(least, tile_least)
    bad = outside_range(total, least)

    @pl.when(bad > 0.0)
    def _():
        own_frames = [(k_ref.at[g], v_ref.at[g], None) for g in range(4)]
        halos = [(halo_key_ref.at[at], halo_ones_ref.at[at], edge_ref[at]) for at in (0, 1)]
        attend_again(
            q_ref, [(0, own_frames[:2] + halos[:1]), (3, own_frames[2:] + halos[1:])], rows_ref
        )

    here = block_means(rows_ref)
    pairs = here[0] + inner_mean_ref[:, :128]
    third = here[1] + inner_mean_ref[:, 128:]
    third = third + pltpu.roll(third, 64, axis=1)
    weight_copy.wait()
    partial = nn_dot(pairs.astype(bf16), weight_ref[:128, :])
    partial += nn_dot(third[:, :64].astype(bf16), weight_ref[128:, :])
    partial_ref[...] = partial.astype(bf16)
    put_products(rows_ref, first_ref, third_ref, out_ref, out_hbm.at[:, 1], sems)


OUT_SCRATCH = [
    pltpu.VMEM((1, 3 * TOKENS, 128), bf16),
    pltpu.VMEM((4, 3 * TOKENS, 128), bf16),
    pltpu.VMEM((192, 768), bf16),
    pltpu.SemaphoreType.DMA((4,)),
]


def attend_inner(q, k, v, weight):
    vmem, hbm = pl.BlockSpec(memory_space=pltpu.VMEM), pl.BlockSpec(memory_space=pltpu.HBM)
    return pl.pallas_call(
        inner_kernel,
        in_specs=[vmem] * 3 + [hbm],
        out_specs=[hbm] + [vmem] * 5,
        out_shape=[
            pltpu.HBM((4, 2, 3 * TOKENS, 128), bf16),
            jax.ShapeDtypeStruct((4, 128, 384), bf16),
            jax.ShapeDtypeStruct((32, 256), f32),
            jax.ShapeDtypeStruct((2, TOKENS, 384), f32),
            jax.ShapeDtypeStruct((2, 256, 512), bf16),
            jax.ShapeDtypeStruct((384, 512), bf16),
        ],
        scratch_shapes=OUT_SCRATCH,
        compiler_params=params(24),
        cost_estimate=cost(10 * 2 * 512 * 320 * 3 * 256, 6e6, 10 * 512 * 320 * 3),
        name="attend_inner",
    )(q, k, v, *in_hbm(weight))


def attend_outer(
    edge, mask, q, k, v, part, first, last, inner_mean, weight, first_weight, third_weight, inner
):
    vmem, hbm = pl.BlockSpec(memory_space=pltpu.VMEM), pl.BlockSpec(memory_space=pltpu.HBM)
    return pl.pallas_call(
        outer_kernel,
        in_specs=[pl.BlockSpec(memory_space=pltpu.SMEM)] + [vmem] * 10 + [hbm] * 2,
        out_specs=[hbm, vmem],
        out_shape=[
            pltpu.HBM((4, 2, 3 * TOKENS, 128), bf16),
            jax.ShapeDtypeStruct((32, 768), bf16),
        ],
        input_output_aliases={12: 0},
        scratch_shapes=[
            pltpu.VMEM((2, 192, TOKENS), bf16),
            pltpu.VMEM((2, TOKENS, 256), bf16),
        ]
        + OUT_SCRATCH,
        compiler_params=params(24),
        cost_estimate=cost(2 * 2 * 512 * 320 * 3 * 256, 6e6, 2 * 512 * 320 * 3),
        name="attend_outer",
    )(
        edge, mask, q, k, v, part, first, last, inner_mean, first_weight, third_weight,
        *in_hbm(weight), inner,
    )


def load_kernel(_, *refs):
    sources, targets, sems = refs[:4], refs[4:8], refs[8]
    copies = [
        pltpu.make_async_copy(source, target, sems.at[i])
        for i, (source, target) in enumerate(zip(sources, targets))
    ]
    for copy in copies:
        copy.start()
    for copy in copies:
        copy.wait()


def load(after, *arrays):
    anywhere = pl.BlockSpec(memory_space=pl.ANY)
    return pl.pallas_call(
        load_kernel,
        in_specs=[anywhere] * 5,
        out_specs=[anywhere] * 4,
        out_shape=[pltpu.VMEM(array.shape, array.dtype) for array in arrays],
        scratch_shapes=[pltpu.SemaphoreType.DMA((4,))],
        compiler_params=params(4),
        cost_estimate=cost(0, 6e6),
        name="load",
    )(after, *in_hbm(*arrays))


def coarse_project_kernel(
    p0, p1, p2, p3, mean_ref, merge_ref, gain_ref, weight_ref, coarse_ref, q_ref, kv_ref
):
    pooled = mean_ref[...] + (
        (p0[...].astype(f32) + p1[...].astype(f32)) + (p2[...].astype(f32) + p3[...].astype(f32))
    )
    coarse = nn_dot(pooled.astype(bf16), merge_ref[...]).astype(bf16)
    coarse_ref[...] = coarse
    wide = coarse.astype(f32)
    scale = lax.rsqrt(jnp.mean(wide * wide, axis=-1, keepdims=True) + EPSILON)
    normed = (wide * scale * gain_ref[...].reshape(1, 1536)).astype(bf16)
    q_ref[...] = (nn_dot(normed, weight_ref[0]) * (128**-0.5 * LOG2E)).astype(bf16)
    key = nn_dot(normed, weight_ref[1]).astype(bf16)
    value = nn_dot(normed, weight_ref[2]).astype(bf16)
    for copy in range(8):
        kv_ref[copy, :, :384] = key
        kv_ref[copy, :, 384:] = value


def coarse_project(partials, mean, merge, gain, weight):
    return pl.pallas_call(
        coarse_project_kernel,
        in_specs=[pl.BlockSpec(memory_space=pltpu.VMEM)] * 8,
        out_specs=[whole(32, 1536), whole(32, 384), whole(8, 32, 768)],
        out_shape=[
            jax.ShapeDtypeStruct((32, 1536), bf16),
            jax.ShapeDtypeStruct((32, 384), bf16),
            pltpu.HBM((8, 32, 768), bf16),
        ],
        compiler_params=params(20),
        cost_estimate=cost(2 * 32 * 1536 * 1920, 7e6),
        name="coarse_project",
    )(*partials, mean, merge, gain, weight)


def coarse_attend_kernel(
    q0, q1, q2, q3, kv_ref, other_ref, split_hbm, o0, o1, o2, o3, split_out, sems
):
    split_copy = pltpu.make_async_copy(split_hbm, split_out, sems.at[0])
    split_copy.start()
    query = jnp.concatenate([ref[...] for ref in (q0, q1, q2, q3)], axis=0)
    outs = (o0, o1, o2, o3)
    lane = lax.broadcasted_iota(jnp.int32, (128, 128), 1)
    stats = jnp.zeros((128, 128), f32)
    for head in range(3):
        lanes = slice(128 * head, 128 * head + 128)
        values = slice(384 + 128 * head, 512 + 128 * head)
        scores = [nt_dot(query[:, lanes], ref[:, lanes]) for ref in (kv_ref, other_ref)]
        top = jnp.max(jnp.maximum(scores[0], scores[1]), axis=-1, keepdims=True)
        weights = [jnp.exp2(score - top) for score in scores]
        total = jnp.sum(weights[0] + weights[1], axis=-1, keepdims=True)
        summed = nn_dot(weights[0].astype(bf16), kv_ref[:, values])
        summed += nn_dot(weights[1].astype(bf16), other_ref[:, values])
        summed = (summed / total).astype(bf16)
        rest = top + jnp.log(total) * LOG2E
        for part in range(3):
            piece = rest.astype(bf16).astype(f32)
            stats = jnp.where(lane == 3 * head + part, piece, stats)
            rest = rest - piece
        for i, out in enumerate(outs):
            out[:, lanes] = summed[32 * i : 32 * i + 32]
    for i, out in enumerate(outs):
        out[:, 384:] = stats[32 * i : 32 * i + 32].astype(bf16)
    split_copy.wait()


def coarse_attend(queries, kv, other, split):
    vmem, anywhere = pl.BlockSpec(memory_space=pltpu.VMEM), pl.BlockSpec(memory_space=pl.ANY)
    return pl.pallas_call(
        coarse_attend_kernel,
        in_specs=[vmem] * 6 + [anywhere],
        out_specs=[vmem] * 4 + [anywhere],
        out_shape=[jax.ShapeDtypeStruct((32, 512), bf16)] * 4 + [pltpu.VMEM(split.shape, bf16)],
        scratch_shapes=[pltpu.SemaphoreType.DMA((1,))],
        compiler_params=params(16),
        cost_estimate=cost(4 * 128 * 512 * 384, 1e6, 128 * 512 * 3),
        name="coarse_attend",
    )(*queries, kv, other, *in_hbm(split))


def coarse_combine_kernel(p0, p1, p2, p3, weight_ref, out_ref):
    parts = (p0, p1, p2, p3)
    heads = []
    for head in range(3):
        lanes = slice(128 * head, 128 * head + 128)
        logs = [
            jnp.sum(part[:, 384 + 3 * head : 387 + 3 * head].astype(f32), axis=-1, keepdims=True)
            for part in parts
        ]
        top = functools.reduce(jnp.maximum, logs)
        shares = [jnp.exp2(log - top) for log in logs]
        summed = sum(share * part[:, lanes].astype(f32) for share, part in zip(shares, parts))
        heads.append((summed / sum(shares)).astype(bf16))
    attended = jnp.concatenate(heads, axis=-1)
    out_ref[...] = nn_dot(attended, weight_ref[...]).astype(bf16)


def coarse_combine(parts, weight):
    return pl.pallas_call(
        coarse_combine_kernel,
        out_shape=jax.ShapeDtypeStruct((32, 1536), bf16),
        compiler_params=params(16),
        cost_estimate=cost(2 * 32 * 384 * 1536, 2e6),
        name="coarse_combine",
    )(*parts, weight)


def split_kernel(
    x_hbm, rows_hbm, coarse_ref, p0, p1, p2, p3, weight_ref, out_hbm,
    x_ref, rows_ref, out_ref, in_sems, out_sems,
):
    x_copy = pltpu.make_async_copy(x_hbm, x_ref, in_sems.at[2])
    x_copy.start()
    in_copies = [
        pltpu.make_async_copy(rows_hbm.at[pair], rows_ref.at[pair], in_sems.at[pair])
        for pair in (0, 1)
    ]
    for copy in in_copies:
        copy.start()
    mixed = (p0[...].astype(f32) + p1[...].astype(f32)) + (
        p2[...].astype(f32) + p3[...].astype(f32)
    )
    after = (coarse_ref[...].astype(f32) + mixed).astype(bf16)
    split = nt_dot(after, weight_ref[...])
    row = lax.broadcasted_iota(jnp.int32, (128, 32), 0)
    col = lax.broadcasted_iota(jnp.int32, (128, 32), 1)
    spread = jnp.where(col == (row >> 5) * 8 + ((row & 31) >> 2), 1.0, 0.0)
    grid = jnp.dot(spread, split, preferred_element_type=f32, precision=lax.Precision.HIGHEST)
    out_copies = []
    x_copy.wait()
    for pair, frames in enumerate(((1, 2), (0, 3))):
        in_copies[pair].wait()
        third = rows_ref[pair, 2 * TOKENS :, :].astype(f32)
        for at, frame in enumerate(frames):
            x = x_ref[frame].astype(f32)
            one = rows_ref[pair, TOKENS * at : TOKENS * (at + 1), :].astype(f32)
            two = pltpu.roll(third, 64, axis=1) if at else third
            for lanes, added in ((slice(0, 128), one), (slice(128, 192), two[:, :64])):
                hidden = (x[:, lanes] + added).astype(bf16).astype(f32)
                hidden = hidden.reshape(4, 4, COLS, -1) + grid[:, lanes].reshape(4, 1, COLS, -1)
                out_ref[frame, :, :, lanes] = hidden.reshape(ROWS, COLS, -1).astype(bf16)
            out_copies.append(
                pltpu.make_async_copy(out_ref.at[frame], out_hbm.at[frame], out_sems.at[frame])
            )
            out_copies[-1].start()
    for copy in out_copies:
        copy.wait()


def split_rows(x, rows, coarse, partials, weight):
    vmem, hbm = pl.BlockSpec(memory_space=pltpu.VMEM), pl.BlockSpec(memory_space=pltpu.HBM)
    return pl.pallas_call(
        split_kernel,
        in_specs=[hbm, hbm] + [vmem] * 6,
        out_specs=hbm,
        out_shape=jax.ShapeDtypeStruct((4, ROWS, COLS, 192), bf16),
        scratch_shapes=[
            pltpu.VMEM((4, TOKENS, 192), bf16),
            pltpu.VMEM((2, 3 * TOKENS, 128), bf16),
            pltpu.VMEM((4, ROWS, COLS, 192), bf16),
            pltpu.SemaphoreType.DMA((3,)),
            pltpu.SemaphoreType.DMA((4,)),
        ],
        compiler_params=params(24),
        cost_estimate=cost(2 * 32 * 1536 * 192, 4e6),
        name="split_rows",
    )(*in_hbm(x, rows), coarse, *partials, weight)


def shifted(value, axis, shift):
    return lax.ppermute(value, axis, [(i, (i + shift) % 4) for i in range(4)])


def from_others(value, axis):
    return [shifted(value, axis, shift) for shift in (1, 2, 3)]


def body(x, fine_gain, fine_qkv, fine_out, merge, coarse_gain, coarse_qkv, coarse_out, split):
    x = x.reshape(4, TOKENS, 768)
    groups = lax.axis_size(FRAMES)
    here = lax.axis_index(FRAMES)
    place = lax.axis_index("mp").astype(jnp.int32).reshape(1)
    edge = jnp.stack(
        [jnp.where(here == 0, 0.0, 1.0), jnp.where(here == groups - 1, 0.0, 1.0)]
    ).astype(f32)

    q, k, v, initial, final, frame_mean, own = fine_project(
        place, x, fine_gain, jnp.transpose(fine_qkv, (1, 2, 0))
    )
    first = lax.ppermute(final, FRAMES, [(i, i + 1) for i in range(groups - 1)])
    last = lax.ppermute(initial, FRAMES, [(i + 1, i) for i in range(groups - 1)])
    inner, mask, inner_mean, part, *weights = attend_inner(q, k, v, fine_out)
    products, partial = attend_outer(
        edge, mask, q, k, v, part, first, last, inner_mean, fine_out, *weights, inner
    )
    partials = from_others(partial, "mp")
    rows = lax.psum_scatter(products, "mp", scatter_dimension=0, tiled=True)
    frame_mean, merge, coarse_qkv, coarse_gain = load(
        partials[0], frame_mean, merge, jnp.transpose(coarse_qkv, (1, 0, 2)), coarse_gain
    )

    coarse, coarse_q, coarse_kv = coarse_project(
        [partial] + partials, frame_mean, merge, coarse_gain, coarse_qkv
    )
    coarse_kv = lax.all_to_all(coarse_kv, "z", 0, 0, tiled=True).reshape(256, 768)
    queries = [coarse_q] + from_others(coarse_q, "x")
    coarse_kv, queries = lax.optimization_barrier((coarse_kv, queries))
    other_kv = lax.ppermute(coarse_kv, "core", [(0, 1), (1, 0)])
    *parts, split = coarse_attend(queries, coarse_kv, other_kv, jnp.transpose(split, (1, 0)))
    parts = parts[:1] + [shifted(parts[s], "x", 4 - s) for s in (1, 2, 3)]
    coarse_partial = coarse_combine(parts, coarse_out)
    coarse_partials = [coarse_partial] + from_others(coarse_partial, "mp")
    return split_rows(
        own, rows.reshape(2, 3 * TOKENS, 128), coarse, coarse_partials, split
    )


def solution(mesh):
    parts = jax.sharding.Mesh(mesh.devices.reshape(4, 8, 2, 4), FRAMES + ("mp",))
    in_specs = (
        P(FRAMES, None, None, None),
        P(),
        P(None, None, "mp"),
        P("mp", None),
        P(),
        P(),
        P(None, None, "mp"),
        P("mp", None),
        P(None, "mp"),
    )
    out_specs = P(FRAMES, None, None, "mp")
    return jax.shard_map(body, mesh=parts, in_specs=in_specs, out_specs=out_specs, check_vma=False)
```

```python
import functools

import jax
import jax.numpy as jnp
from jax import lax
from jax.experimental import pallas as pl
from jax.experimental.pallas import tpu as pltpu
from jax.sharding import PartitionSpec as P

HEADS = 12
EPSILON = 1e-06
REACH = 3
LOG2E = 1.4426950408889634
ROWS, COLS = 16, 32
TOKENS = ROWS * COLS
FRAMES = ("x", "far", "near", "core")
MIB = 1 << 20
bf16, f32 = jnp.bfloat16, jnp.float32


def nt_dot(a, b):
    return lax.dot_general(a, b, (((1,), (1,)), ((), ())), preferred_element_type=f32)


def nn_dot(a, b):
    return jnp.dot(a, b, preferred_element_type=f32)


def block_mean_matrix(rows):
    token = lax.broadcasted_iota(jnp.int32, (32, rows * COLS), 1)
    block = lax.broadcasted_iota(jnp.int32, (32, rows * COLS), 0)
    of_token = token // (rows * COLS // 4) * 8 + ((token & 31) >> 2)
    return jnp.where(of_token == block, 1.0 / 64, 0.0)


def params(mib):
    return pltpu.CompilerParams(vmem_limit_bytes=mib * MIB)


def cost(flops, bytes_accessed, transcendentals=0):
    return pl.CostEstimate(
        flops=int(flops), bytes_accessed=int(bytes_accessed), transcendentals=int(transcendentals)
    )


def whole(*shape):
    return pl.BlockSpec(shape, lambda *i: (0,) * len(shape))


def fine_project_kernel(
    place_ref, x_hbm, gain_hbm, weight_hbm,
    q_ref, key_ref, ones_ref, initial_hbm, last_hbm, mean_hbm, own_hbm,
    x_ref, gain_ref, weight_ref, rows_ref, sum_ref, edge_ref, own_ref, mean_ref,
    in_sems, out_sems,
):
    gain_copy = pltpu.make_async_copy(gain_hbm, gain_ref, in_sems.at[5])
    gain_copy.start()
    weight_copy = pltpu.make_async_copy(weight_hbm, weight_ref, in_sems.at[4])
    weight_copy.start()
    x_copies = [
        pltpu.make_async_copy(x_hbm.at[frame], x_ref.at[frame], in_sems.at[frame])
        for frame in range(4)
    ]
    order = (0, 3, 1, 2)
    for frame in order:
        x_copies[frame].start()
    gain_copy.wait()
    weight_copy.wait()
    gain = gain_ref[...].reshape(1, 768)
    query, key, value = (weight_ref[i].astype(f32) * gain for i in range(3))
    rows_ref[:192, :] = value.astype(bf16)
    rows_ref[192:384, :] = key.astype(bf16)
    rows_ref[384:, :] = (query * (0.125 * LOG2E)).astype(bf16)

    out_copies = [
        pltpu.make_async_copy(edge_ref.at[i], out, out_sems.at[i])
        for i, out in enumerate((initial_hbm, last_hbm))
    ]

    for step, frame in enumerate(order):
        x_copies[frame].wait()
        if step == 3:
            for place in range(4):

                @pl.when(place_ref[0] == place)
                def _():
                    own_ref[...] = x_ref[:, :, 192 * place : 192 * place + 192]

            out_copies.append(pltpu.make_async_copy(own_ref, own_hbm, out_sems.at[2]))
            out_copies[-1].start()
        x = x_ref[frame]
        wide = x.astype(f32)
        projected = nt_dot(x, rows_ref[...])
        scale = lax.rsqrt(jnp.mean(wide * wide, axis=-1, keepdims=True) + EPSILON)
        projected = projected * scale
        q_ref[frame] = projected[:, 384:].astype(bf16)
        pairs = projected[:, :384]
        lane = lax.broadcasted_iota(jnp.int32, (1, 256), 1)
        ones_ref[frame] = jnp.where(lane < 192, projected[:, :256], 1.0).astype(bf16)
        along = jnp.transpose(jnp.broadcast_to(scale, (TOKENS, 128)))[:1]
        key_ref[frame] = (nt_dot(rows_ref[192:384, :], x) * along).astype(bf16)
        added = jnp.sum(wide.reshape(4, 4, COLS, 768), axis=1).reshape(4 * COLS, 768)
        sum_ref[...] = sum_ref[...] + added if step else added
        if step < 2:
            edge_ref[step] = pairs.astype(bf16)
            out_copies[step].start()
    mean_ref[...] = jnp.dot(
        block_mean_matrix(4),
        sum_ref[...],
        preferred_element_type=f32,
        precision=lax.Precision.HIGHEST,
    )
    out_copies.append(pltpu.make_async_copy(mean_ref, mean_hbm, out_sems.at[3]))
    out_copies[-1].start()
    for copy in out_copies:
        copy.wait()


def in_hbm(*arrays):
    return [pltpu.with_memory_space_constraint(array, pltpu.HBM) for array in arrays]


def fine_project(place, x, gain, weight):
    vmem, hbm = pl.BlockSpec(memory_space=pltpu.VMEM), pl.BlockSpec(memory_space=pltpu.HBM)
    return pl.pallas_call(
        fine_project_kernel,
        in_specs=[pl.BlockSpec(memory_space=pltpu.SMEM), hbm, hbm, hbm],
        out_specs=[vmem, vmem, vmem, hbm, hbm, hbm, hbm],
        out_shape=[
            jax.ShapeDtypeStruct((4, TOKENS, 192), bf16),
            jax.ShapeDtypeStruct((4, 192, TOKENS), bf16),
            jax.ShapeDtypeStruct((4, TOKENS, 256), bf16),
            pltpu.HBM((TOKENS, 384), bf16),
            pltpu.HBM((TOKENS, 384), bf16),
            pltpu.HBM((32, 768), f32),
            pltpu.HBM((4, TOKENS, 192), bf16),
        ],
        scratch_shapes=[
            pltpu.VMEM((4, TOKENS, 768), bf16),
            pltpu.VMEM((768,), f32),
            pltpu.VMEM((3, 192, 768), bf16),
            pltpu.VMEM((576, 768), bf16),
            pltpu.VMEM((128, 768), f32),
            pltpu.VMEM((2, TOKENS, 384), bf16),
            pltpu.VMEM((4, TOKENS, 192), bf16),
            pltpu.VMEM((32, 768), f32),
            pltpu.SemaphoreType.DMA((6,)),
            pltpu.SemaphoreType.DMA((4,)),
        ],
        compiler_params=params(24),
        cost_estimate=cost(2 * 2048 * 768 * 768, 8e6),
        name="fine_project",
    )(place, *in_hbm(x, gain, weight))


BASES = (0, 0, 128, 128)
WINDOWS = ((0, 256), (0, 384), (128, 512), (256, 512))


def near_keys(tile, base):
    query = lax.broadcasted_iota(jnp.int32, (128, 384), 0) + 128 * tile
    key = lax.broadcasted_iota(jnp.int32, (128, 384), 1) + base
    rows = jnp.abs((query >> 5) - (key >> 5))
    cols = jnp.abs((query & 31) - (key & 31))
    return (rows <= REACH) & (cols <= REACH)


def outside_range(total, least):
    low = lax.broadcasted_iota(jnp.int32, (128, 128), 1) < 64
    bad = jnp.where((total < 2.0**60) & (least > 2.0**-60), 0.0, 1.0)
    return jnp.max(jnp.where(low, bad, 0.0))


def rows_at(part, tile):
    start = part * TOKENS + tile * 128
    return pl.ds(start if isinstance(start, int) else pl.multiple_of(start, 128), 128)


def window_of(tile):
    base = pl.multiple_of((tile >> 1) * 128, 128)
    return base, pl.ds(base, 384), pl.ds(pl.multiple_of(tile * 128, 128), 128)


def put_rows(out_ref, tile, pair):
    low = lax.broadcasted_iota(jnp.int32, (128, 128), 1) < 64
    thirds, counts = [], []
    for at, sums in enumerate(pair):
        turned = [pltpu.roll(one, 64, axis=1) for one in sums]
        heads = [one / other for one, other in zip(sums, turned)]
        out_ref[0, rows_at(at, tile), :] = jnp.where(
            low, heads[0], heads[1]
        ).astype(bf16)
        thirds.append(heads[2])
        counts += [turned[0], sums[1], turned[2]]
    packed = jnp.where(low, thirds[0], pltpu.roll(thirds[1], 64, axis=1))
    out_ref[0, rows_at(2, tile), :] = packed.astype(bf16)
    return sum(counts), functools.reduce(jnp.minimum, counts)


def stack_heads(query):
    head = lax.broadcasted_iota(jnp.int32, (1, 192), 1) >> 6
    return jnp.concatenate(
        [query * jnp.where(head == i, 1.0, 0.0).astype(bf16) for i in range(3)], axis=0
    )


def own_parts(summed):
    low = lax.broadcasted_iota(jnp.int32, (1, 128, 128), 2) < 64
    first, second = summed[..., :128], summed[..., 128:]
    n = summed.shape[1]
    turned = pltpu.roll(second[1].reshape(n * 128, 128), 64, axis=1).reshape(n, 128, 128)
    return [
        jnp.where(low, first[0], second[0]),
        jnp.where(low, turned, first[1]),
        second[2],
    ]


def attend_again(q_ref, frames, out_ref):
    def redo(tile, _):
        base, window, own = window_of(tile)
        near = jnp.concatenate([near_keys(tile, base)] * 3, axis=0)
        pair = []
        for frame, sources in frames:
            query = stack_heads(q_ref[frame, own, :])
            scores = []
            for keys, _, inside in sources:
                seen = near if inside is None else near & (inside > 0.0)
                scores.append(jnp.where(seen, nn_dot(query, keys[:, window]), -jnp.inf))
            top = jnp.max(
                jnp.maximum(jnp.maximum(scores[0], scores[1]), scores[2]), axis=-1, keepdims=True
            )
            summed = sum(
                nn_dot(jnp.exp2(score - top).astype(bf16), ones[window, :])
                for score, (_, ones, _) in zip(scores, sources)
            )
            pair.append([part[0] for part in own_parts(summed.reshape(3, 1, 128, 256))])
        put_rows(out_ref, tile, pair)
        return 0

    lax.fori_loop(0, 4, redo, 0)


def weigh(query, keys, ones, mask):
    n = query.shape[0]
    weights = jnp.exp2(nn_dot(stack_heads(query.reshape(n * 128, 192)), keys)).astype(bf16)
    weights = (weights.reshape(3 * n, *mask.shape) * mask[None]).reshape(-1, mask.shape[1])
    return own_parts(nn_dot(weights, ones).reshape(3, n, 128, 256))


def tiles():
    for tile in range(4):
        first, last = WINDOWS[tile]
        own = slice(128 * tile, 128 * tile + 128)
        yield tile, own, slice(first, last), slice(first - BASES[tile], last - BASES[tile])


def block_means(out_ref):
    matrix = block_mean_matrix(ROWS).astype(bf16)
    pairs = nn_dot(matrix, out_ref[0, :TOKENS, :])
    pairs += nn_dot(matrix, out_ref[0, TOKENS : 2 * TOKENS, :])
    return pairs, nn_dot(matrix, out_ref[0, 2 * TOKENS :, :])


def set_weights(weight_ref, first_ref, third_ref):
    first_ref[...] = jnp.zeros_like(first_ref)
    third_ref[...] = jnp.zeros_like(third_ref)
    for place in range(4):
        weight = weight_ref[:, 192 * place : 192 * place + 192]
        lanes = slice(128 * place, 128 * place + 128)
        for at in (0, 1):
            first_ref[at, :128, lanes] = weight[:128, :128]
            first_ref[at, 128 + 64 * at : 192 + 64 * at, lanes] = weight[128:, :128]
            half = slice(128 * place + 64 * at, 128 * place + 64 * at + 64)
            third_ref[128 * at : 128 * at + 128, half] = weight[:128, 128:]
            third_ref[256 + 64 * at : 320 + 64 * at, half] = weight[128:, 128:]


def put_products(rows_ref, first_ref, third_ref, out_ref, out_hbm, sems):
    parts = [rows_ref[0, TOKENS * i : TOKENS * (i + 1), :] for i in range(3)]
    copies = []
    for i in range(3):
        if i < 2:
            product = nn_dot(jnp.concatenate([parts[i], parts[2]], axis=1), first_ref[i])
        else:
            product = nn_dot(jnp.concatenate(parts, axis=1), third_ref[...])
        own = pl.ds(TOKENS * i, TOKENS)
        for place in range(4):
            out_ref[place, own, :] = product[:, 128 * place : 128 * place + 128].astype(bf16)
        copies.append(
            pltpu.make_async_copy(out_ref.at[:, own, :], out_hbm.at[:, own, :], sems.at[i])
        )
        copies[-1].start()
    for copy in copies:
        copy.wait()


def inner_kernel(
    q_ref, k_ref, v_ref, weight_hbm,
    out_hbm, mask_ref, mean_ref, part_ref, first_ref, third_ref, rows_ref, out_ref, weight_ref, sems,
):
    weight_copy = pltpu.make_async_copy(weight_hbm, weight_ref, sems.at[3])
    weight_copy.start()

    total, least = jnp.zeros((128, 128), f32), jnp.ones((128, 128), f32)
    for tile, own, window, seen in tiles():
        mask_ref[tile] = jnp.where(near_keys(tile, BASES[tile]), 1.0, 0.0).astype(bf16)
        sums = [None] * 4
        for g in range(4):
            lo, hi = max(g - 1, 0), min(g + 1, 3)
            parts = weigh(
                q_ref[lo : hi + 1, own, :],
                k_ref[g, :, window],
                v_ref[g, window, :],
                mask_ref[tile, :, seen],
            )
            for f in range(lo, hi + 1):
                here = [part[f - lo] for part in parts]
                sums[f] = here if sums[f] is None else [a + b for a, b in zip(sums[f], here)]
        for head in range(3):
            lanes = slice(128 * head, 128 * head + 128)
            part_ref[0, own, lanes] = sums[0][head]
            part_ref[1, own, lanes] = sums[3][head]
        tile_total, tile_least = put_rows(rows_ref, tile, sums[1:3])
        total, least = total + tile_total, jnp.minimum(least, tile_least)
    bad = outside_range(total, least)

    @pl.when(bad > 0.0)
    def _():
        own_frames = [(k_ref.at[g], v_ref.at[g], None) for g in range(4)]
        attend_again(q_ref, [(1, own_frames[:3]), (2, own_frames[1:])], rows_ref)

    mean_ref[:, :128], mean_ref[:, 128:] = block_means(rows_ref)
    weight_copy.wait()
    set_weights(weight_ref, first_ref, third_ref)
    put_products(rows_ref, first_ref, third_ref, out_ref, out_hbm.at[:, 0], sems)


def outer_kernel(
    edge_ref, mask_ref, q_ref, k_ref, v_ref, part_ref, halo_first_ref, halo_last_ref,
    inner_mean_ref, first_ref, third_ref, weight_hbm, inner_ref,
    out_hbm, partial_ref, halo_key_ref, halo_ones_ref,
    rows_ref, out_ref, weight_ref, sems,
):
    weight_copy = pltpu.make_async_copy(weight_hbm, weight_ref, sems.at[3])
    weight_copy.start()
    lane = lax.broadcasted_iota(jnp.int32, (1, 256), 1)
    for at, halo_ref in enumerate((halo_first_ref, halo_last_ref)):
        halo = halo_ref[...].astype(f32)
        halo_ones_ref[at] = (jnp.where(lane < 192, halo[:, :256], 1.0) * edge_ref[at]).astype(bf16)
        halo_key_ref[at] = jnp.transpose(halo)[192:].astype(bf16)

    total, least = jnp.zeros((128, 128), f32), jnp.ones((128, 128), f32)
    for tile, own, window, seen in tiles():
        pair = []
        for at, frame in enumerate((0, 3)):
            more = weigh(
                q_ref[frame : frame + 1, own, :],
                halo_key_ref[at, :, window],
                halo_ones_ref[at, window, :],
                mask_ref[tile, :, seen],
            )
            pair.append(
                [
                    part_ref[at, own, 128 * head : 128 * head + 128] + more[head][0]
                    for head in range(3)
                ]
            )
        tile_total, tile_least = put_rows(rows_ref, tile, pair)
        total, least = total + tile_total, jnp.minimum(least, tile_least)
    bad = outside_range(total, least)

    @pl.when(bad > 0.0)
    def _():
        own_frames = [(k_ref.at[g], v_ref.at[g], None) for g in range(4)]
        halos = [(halo_key_ref.at[at], halo_ones_ref.at[at], edge_ref[at]) for at in (0, 1)]
        attend_again(
            q_ref, [(0, own_frames[:2] + halos[:1]), (3, own_frames[2:] + halos[1:])], rows_ref
        )

    here = block_means(rows_ref)
    pairs = here[0] + inner_mean_ref[:, :128]
    third = here[1] + inner_mean_ref[:, 128:]
    third = third + pltpu.roll(third, 64, axis=1)
    weight_copy.wait()
    partial = nn_dot(pairs.astype(bf16), weight_ref[:128, :])
    partial += nn_dot(third[:, :64].astype(bf16), weight_ref[128:, :])
    partial_ref[...] = partial.astype(bf16)
    put_products(rows_ref, first_ref, third_ref, out_ref, out_hbm.at[:, 1], sems)


OUT_SCRATCH = [
    pltpu.VMEM((1, 3 * TOKENS, 128), bf16),
    pltpu.VMEM((4, 3 * TOKENS, 128), bf16),
    pltpu.VMEM((192, 768), bf16),
    pltpu.SemaphoreType.DMA((4,)),
]


def attend_inner(q, k, v, weight):
    vmem, hbm = pl.BlockSpec(memory_space=pltpu.VMEM), pl.BlockSpec(memory_space=pltpu.HBM)
    return pl.pallas_call(
        inner_kernel,
        in_specs=[vmem] * 3 + [hbm],
        out_specs=[hbm] + [vmem] * 5,
        out_shape=[
            pltpu.HBM((4, 2, 3 * TOKENS, 128), bf16),
            jax.ShapeDtypeStruct((4, 128, 384), bf16),
            jax.ShapeDtypeStruct((32, 256), f32),
            jax.ShapeDtypeStruct((2, TOKENS, 384), f32),
            jax.ShapeDtypeStruct((2, 256, 512), bf16),
            jax.ShapeDtypeStruct((384, 512), bf16),
        ],
        scratch_shapes=OUT_SCRATCH,
        compiler_params=params(24),
        cost_estimate=cost(10 * 2 * 512 * 320 * 3 * 256, 6e6, 10 * 512 * 320 * 3),
        name="attend_inner",
    )(q, k, v, *in_hbm(weight))


def attend_outer(
    edge, mask, q, k, v, part, first, last, inner_mean, weight, first_weight, third_weight, inner
):
    vmem, hbm = pl.BlockSpec(memory_space=pltpu.VMEM), pl.BlockSpec(memory_space=pltpu.HBM)
    return pl.pallas_call(
        outer_kernel,
        in_specs=[pl.BlockSpec(memory_space=pltpu.SMEM)] + [vmem] * 10 + [hbm] * 2,
        out_specs=[hbm, vmem],
        out_shape=[
            pltpu.HBM((4, 2, 3 * TOKENS, 128), bf16),
            jax.ShapeDtypeStruct((32, 768), bf16),
        ],
        input_output_aliases={12: 0},
        scratch_shapes=[
            pltpu.VMEM((2, 192, TOKENS), bf16),
            pltpu.VMEM((2, TOKENS, 256), bf16),
        ]
        + OUT_SCRATCH,
        compiler_params=params(24),
        cost_estimate=cost(2 * 2 * 512 * 320 * 3 * 256, 6e6, 2 * 512 * 320 * 3),
        name="attend_outer",
    )(
        edge, mask, q, k, v, part, first, last, inner_mean, first_weight, third_weight,
        *in_hbm(weight), inner,
    )


def load_kernel(_, *refs):
    sources, targets, sems = refs[:4], refs[4:8], refs[8]
    copies = [
        pltpu.make_async_copy(source, target, sems.at[i])
        for i, (source, target) in enumerate(zip(sources, targets))
    ]
    for copy in copies:
        copy.start()
    for copy in copies:
        copy.wait()


def load(after, *arrays):
    anywhere = pl.BlockSpec(memory_space=pl.ANY)
    return pl.pallas_call(
        load_kernel,
        in_specs=[anywhere] * 5,
        out_specs=[anywhere] * 4,
        out_shape=[pltpu.VMEM(array.shape, array.dtype) for array in arrays],
        scratch_shapes=[pltpu.SemaphoreType.DMA((4,))],
        compiler_params=params(4),
        cost_estimate=cost(0, 6e6),
        name="load",
    )(after, *in_hbm(*arrays))


def coarse_project_kernel(
    p0, p1, p2, p3, mean_ref, merge_ref, gain_ref, weight_ref, coarse_ref, q_ref, kv_ref
):
    pooled = mean_ref[...] + (
        (p0[...].astype(f32) + p1[...].astype(f32)) + (p2[...].astype(f32) + p3[...].astype(f32))
    )
    coarse = nn_dot(pooled.astype(bf16), merge_ref[...]).astype(bf16)
    coarse_ref[...] = coarse
    wide = coarse.astype(f32)
    scale = lax.rsqrt(jnp.mean(wide * wide, axis=-1, keepdims=True) + EPSILON)
    normed = (wide * scale * gain_ref[...].reshape(1, 1536)).astype(bf16)
    q_ref[...] = (nn_dot(normed, weight_ref[0]) * (128**-0.5 * LOG2E)).astype(bf16)
    key = nn_dot(normed, weight_ref[1]).astype(bf16)
    value = nn_dot(normed, weight_ref[2]).astype(bf16)
    for copy in range(8):
        kv_ref[copy, :, :384] = key
        kv_ref[copy, :, 384:] = value


def coarse_project(partials, mean, merge, gain, weight):
    return pl.pallas_call(
        coarse_project_kernel,
        in_specs=[pl.BlockSpec(memory_space=pltpu.VMEM)] * 8,
        out_specs=[whole(32, 1536), whole(32, 384), whole(8, 32, 768)],
        out_shape=[
            jax.ShapeDtypeStruct((32, 1536), bf16),
            jax.ShapeDtypeStruct((32, 384), bf16),
            pltpu.HBM((8, 32, 768), bf16),
        ],
        compiler_params=params(20),
        cost_estimate=cost(2 * 32 * 1536 * 1920, 7e6),
        name="coarse_project",
    )(*partials, mean, merge, gain, weight)


def coarse_attend_kernel(
    q0, q1, q2, q3, kv_ref, other_ref, split_hbm, o0, o1, o2, o3, split_out, sems
):
    split_copy = pltpu.make_async_copy(split_hbm, split_out, sems.at[0])
    split_copy.start()
    query = jnp.concatenate([ref[...] for ref in (q0, q1, q2, q3)], axis=0)
    outs = (o0, o1, o2, o3)
    lane = lax.broadcasted_iota(jnp.int32, (128, 128), 1)
    stats = jnp.zeros((128, 128), f32)
    for head in range(3):
        lanes = slice(128 * head, 128 * head + 128)
        values = slice(384 + 128 * head, 512 + 128 * head)
        scores = [nt_dot(query[:, lanes], ref[:, lanes]) for ref in (kv_ref, other_ref)]
        top = jnp.max(jnp.maximum(scores[0], scores[1]), axis=-1, keepdims=True)
        weights = [jnp.exp2(score - top) for score in scores]
        total = jnp.sum(weights[0] + weights[1], axis=-1, keepdims=True)
        summed = nn_dot(weights[0].astype(bf16), kv_ref[:, values])
        summed += nn_dot(weights[1].astype(bf16), other_ref[:, values])
        summed = (summed / total).astype(bf16)
        rest = top + jnp.log(total) * LOG2E
        for part in range(3):
            piece = rest.astype(bf16).astype(f32)
            stats = jnp.where(lane == 3 * head + part, piece, stats)
            rest = rest - piece
        for i, out in enumerate(outs):
            out[:, lanes] = summed[32 * i : 32 * i + 32]
    for i, out in enumerate(outs):
        out[:, 384:] = stats[32 * i : 32 * i + 32].astype(bf16)
    split_copy.wait()


def coarse_attend(queries, kv, other, split):
    vmem, anywhere = pl.BlockSpec(memory_space=pltpu.VMEM), pl.BlockSpec(memory_space=pl.ANY)
    return pl.pallas_call(
        coarse_attend_kernel,
        in_specs=[vmem] * 6 + [anywhere],
        out_specs=[vmem] * 4 + [anywhere],
        out_shape=[jax.ShapeDtypeStruct((32, 512), bf16)] * 4 + [pltpu.VMEM(split.shape, bf16)],
        scratch_shapes=[pltpu.SemaphoreType.DMA((1,))],
        compiler_params=params(16),
        cost_estimate=cost(4 * 128 * 512 * 384, 1e6, 128 * 512 * 3),
        name="coarse_attend",
    )(*queries, kv, other, *in_hbm(split))


def coarse_combine_kernel(p0, p1, p2, p3, weight_ref, out_ref):
    parts = (p0, p1, p2, p3)
    heads = []
    for head in range(3):
        lanes = slice(128 * head, 128 * head + 128)
        logs = [
            jnp.sum(part[:, 384 + 3 * head : 387 + 3 * head].astype(f32), axis=-1, keepdims=True)
            for part in parts
        ]
        top = functools.reduce(jnp.maximum, logs)
        shares = [jnp.exp2(log - top) for log in logs]
        summed = sum(share * part[:, lanes].astype(f32) for share, part in zip(shares, parts))
        heads.append((summed / sum(shares)).astype(bf16))
    attended = jnp.concatenate(heads, axis=-1)
    out_ref[...] = nn_dot(attended, weight_ref[...]).astype(bf16)


def coarse_combine(parts, weight):
    return pl.pallas_call(
        coarse_combine_kernel,
        out_shape=jax.ShapeDtypeStruct((32, 1536), bf16),
        compiler_params=params(16),
        cost_estimate=cost(2 * 32 * 384 * 1536, 2e6),
        name="coarse_combine",
    )(*parts, weight)


def split_kernel(
    x_hbm, rows_hbm, coarse_ref, p0, p1, p2, p3, weight_ref, out_hbm,
    x_ref, rows_ref, out_ref, in_sems, out_sems,
):
    x_copy = pltpu.make_async_copy(x_hbm, x_ref, in_sems.at[2])
    x_copy.start()
    in_copies = [
        pltpu.make_async_copy(rows_hbm.at[pair], rows_ref.at[pair], in_sems.at[pair])
        for pair in (0, 1)
    ]
    for copy in in_copies:
        copy.start()
    mixed = (p0[...].astype(f32) + p1[...].astype(f32)) + (
        p2[...].astype(f32) + p3[...].astype(f32)
    )
    after = (coarse_ref[...].astype(f32) + mixed).astype(bf16)
    split = nt_dot(after, weight_ref[...])
    row = lax.broadcasted_iota(jnp.int32, (128, 32), 0)
    col = lax.broadcasted_iota(jnp.int32, (128, 32), 1)
    spread = jnp.where(col == (row >> 5) * 8 + ((row & 31) >> 2), 1.0, 0.0)
    grid = jnp.dot(spread, split, preferred_element_type=f32, precision=lax.Precision.HIGHEST)
    out_copies = []
    x_copy.wait()
    for pair, frames in enumerate(((1, 2), (0, 3))):
        in_copies[pair].wait()
        third = rows_ref[pair, 2 * TOKENS :, :].astype(f32)
        for at, frame in enumerate(frames):
            x = x_ref[frame].astype(f32)
            one = rows_ref[pair, TOKENS * at : TOKENS * (at + 1), :].astype(f32)
            two = pltpu.roll(third, 64, axis=1) if at else third
            for lanes, added in ((slice(0, 128), one), (slice(128, 192), two[:, :64])):
                hidden = (x[:, lanes] + added).astype(bf16).astype(f32)
                hidden = hidden.reshape(4, 4, COLS, -1) + grid[:, lanes].reshape(4, 1, COLS, -1)
                out_ref[frame, :, :, lanes] = hidden.reshape(ROWS, COLS, -1).astype(bf16)
            out_copies.append(
                pltpu.make_async_copy(out_ref.at[frame], out_hbm.at[frame], out_sems.at[frame])
            )
            out_copies[-1].start()
    for copy in out_copies:
        copy.wait()


def split_rows(x, rows, coarse, partials, weight):
    vmem, hbm = pl.BlockSpec(memory_space=pltpu.VMEM), pl.BlockSpec(memory_space=pltpu.HBM)
    return pl.pallas_call(
        split_kernel,
        in_specs=[hbm, hbm] + [vmem] * 6,
        out_specs=hbm,
        out_shape=jax.ShapeDtypeStruct((4, ROWS, COLS, 192), bf16),
        scratch_shapes=[
            pltpu.VMEM((4, TOKENS, 192), bf16),
            pltpu.VMEM((2, 3 * TOKENS, 128), bf16),
            pltpu.VMEM((4, ROWS, COLS, 192), bf16),
            pltpu.SemaphoreType.DMA((3,)),
            pltpu.SemaphoreType.DMA((4,)),
        ],
        compiler_params=params(24),
        cost_estimate=cost(2 * 32 * 1536 * 192, 4e6),
        name="split_rows",
    )(*in_hbm(x, rows), coarse, *partials, weight)


def shifted(value, axis, shift):
    return lax.ppermute(value, axis, [(i, (i + shift) % 4) for i in range(4)])


def from_others(value, axis):
    return [shifted(value, axis, shift) for shift in (1, 2, 3)]


def body(x, fine_gain, fine_qkv, fine_out, merge, coarse_gain, coarse_qkv, coarse_out, split):
    x = x.reshape(4, TOKENS, 768)
    groups = lax.axis_size(FRAMES)
    here = lax.axis_index(FRAMES)
    place = lax.axis_index("mp").astype(jnp.int32).reshape(1)
    edge = jnp.stack(
        [jnp.where(here == 0, 0.0, 1.0), jnp.where(here == groups - 1, 0.0, 1.0)]
    ).astype(f32)

    q, k, v, initial, final, frame_mean, own = fine_project(
        place, x, fine_gain, jnp.transpose(fine_qkv, (1, 2, 0))
    )
    first = lax.ppermute(final, FRAMES, [(i, i + 1) for i in range(groups - 1)])
    last = lax.ppermute(initial, FRAMES, [(i + 1, i) for i in range(groups - 1)])
    inner, mask, inner_mean, part, *weights = attend_inner(q, k, v, fine_out)
    products, partial = attend_outer(
        edge, mask, q, k, v, part, first, last, inner_mean, fine_out, *weights, inner
    )
    partials = from_others(partial, "mp")
    rows = lax.psum_scatter(products, "mp", scatter_dimension=0, tiled=True)
    frame_mean, merge, coarse_qkv, coarse_gain = load(
        partials[0], frame_mean, merge, jnp.transpose(coarse_qkv, (1, 0, 2)), coarse_gain
    )

    coarse, coarse_q, coarse_kv = coarse_project(
        [partial] + partials, frame_mean, merge, coarse_gain, coarse_qkv
    )
    coarse_kv = lax.all_to_all(coarse_kv, ("x", "near"), 0, 0, tiled=True).reshape(256, 768)
    queries = [coarse_q] + from_others(coarse_q, "far")
    coarse_kv, queries = lax.optimization_barrier((coarse_kv, queries))
    other_kv = lax.ppermute(coarse_kv, "core", [(0, 1), (1, 0)])
    *parts, split = coarse_attend(queries, coarse_kv, other_kv, jnp.transpose(split, (1, 0)))
    parts = parts[:1] + [shifted(parts[s], "far", 4 - s) for s in (1, 2, 3)]
    coarse_partial = coarse_combine(parts, coarse_out)
    coarse_partials = [coarse_partial] + from_others(coarse_partial, "mp")
    return split_rows(
        own, rows.reshape(2, 3 * TOKENS, 128), coarse, coarse_partials, split
    )


def solution(mesh):
    parts = jax.sharding.Mesh(mesh.devices.reshape(4, 4, 2, 2, 4), FRAMES + ("mp",))
    in_specs = (
        P(FRAMES, None, None, None),
        P(),
        P(None, None, "mp"),
        P("mp", None),
        P(),
        P(),
        P(None, None, "mp"),
        P("mp", None),
        P(None, "mp"),
    )
    out_specs = P(FRAMES, None, None, "mp")
    return jax.shard_map(body, mesh=parts, in_specs=in_specs, out_specs=out_specs, check_vma=False)
```

```python
import functools

import jax
import jax.numpy as jnp
from jax import lax
from jax.experimental import pallas as pl
from jax.experimental.pallas import tpu as pltpu
from jax.sharding import PartitionSpec as P

HEADS = 12
EPSILON = 1e-06
REACH = 3
LOG2E = 1.4426950408889634
ROWS, COLS = 16, 32
TOKENS = ROWS * COLS
FRAMES = ("x", "z", "core")
MIB = 1 << 20
bf16, f32 = jnp.bfloat16, jnp.float32


def nt_dot(a, b):
    return lax.dot_general(a, b, (((1,), (1,)), ((), ())), preferred_element_type=f32)


def nn_dot(a, b):
    return jnp.dot(a, b, preferred_element_type=f32)


def block_mean_matrix(rows):
    token = lax.broadcasted_iota(jnp.int32, (32, rows * COLS), 1)
    block = lax.broadcasted_iota(jnp.int32, (32, rows * COLS), 0)
    of_token = token // (rows * COLS // 4) * 8 + ((token & 31) >> 2)
    return jnp.where(of_token == block, 1.0 / 64, 0.0)


def params(mib):
    return pltpu.CompilerParams(vmem_limit_bytes=mib * MIB)


def cost(flops, bytes_accessed, transcendentals=0):
    return pl.CostEstimate(
        flops=int(flops), bytes_accessed=int(bytes_accessed), transcendentals=int(transcendentals)
    )


def whole(*shape):
    return pl.BlockSpec(shape, lambda *i: (0,) * len(shape))


def fine_project_kernel(
    place_ref, x_hbm, gain_hbm, weight_hbm,
    q_ref, key_ref, ones_ref, initial_hbm, last_hbm, mean_hbm, own_hbm,
    x_ref, gain_ref, weight_ref, rows_ref, sum_ref, edge_ref, own_ref, mean_ref,
    in_sems, out_sems,
):
    gain_copy = pltpu.make_async_copy(gain_hbm, gain_ref, in_sems.at[5])
    gain_copy.start()
    weight_copy = pltpu.make_async_copy(weight_hbm, weight_ref, in_sems.at[4])
    weight_copy.start()
    x_copies = [
        pltpu.make_async_copy(x_hbm.at[frame], x_ref.at[frame], in_sems.at[frame])
        for frame in range(4)
    ]
    order = (0, 3, 1, 2)
    for frame in order:
        x_copies[frame].start()
    gain_copy.wait()
    weight_copy.wait()
    gain = gain_ref[...].reshape(1, 768)
    query, key, value = (weight_ref[i].astype(f32) * gain for i in range(3))
    rows_ref[:192, :] = value.astype(bf16)
    rows_ref[192:384, :] = key.astype(bf16)
    rows_ref[384:, :] = (query * (0.125 * LOG2E)).astype(bf16)

    out_copies = [
        pltpu.make_async_copy(edge_ref.at[i], out, out_sems.at[i])
        for i, out in enumerate((initial_hbm, last_hbm))
    ]

    for step, frame in enumerate(order):
        x_copies[frame].wait()
        if step == 3:
            for place in range(4):

                @pl.when(place_ref[0] == place)
                def _():
                    own_ref[...] = x_ref[:, :, 192 * place : 192 * place + 192]

            out_copies.append(pltpu.make_async_copy(own_ref, own_hbm, out_sems.at[2]))
            out_copies[-1].start()
        x = x_ref[frame]
        wide = x.astype(f32)
        added = jnp.sum(wide.reshape(4, 4, COLS, 768), axis=1).reshape(4 * COLS, 768)
        sum_ref[...] = sum_ref[...] + added if step else added
        if step == 3:
            mean_ref[...] = jnp.dot(
                block_mean_matrix(4),
                sum_ref[...],
                preferred_element_type=f32,
                precision=lax.Precision.HIGHEST,
            )
            out_copies.append(pltpu.make_async_copy(mean_ref, mean_hbm, out_sems.at[3]))
            out_copies[-1].start()
        projected = nt_dot(x, rows_ref[...])
        scale = lax.rsqrt(jnp.mean(wide * wide, axis=-1, keepdims=True) + EPSILON)
        projected = projected * scale
        q_ref[frame] = projected[:, 384:].astype(bf16)
        pairs = projected[:, :384]
        lane = lax.broadcasted_iota(jnp.int32, (1, 256), 1)
        ones_ref[frame] = jnp.where(lane < 192, projected[:, :256], 1.0).astype(bf16)
        along = jnp.transpose(jnp.broadcast_to(scale, (TOKENS, 128)))[:1]
        key_ref[frame] = (nt_dot(rows_ref[192:384, :], x) * along).astype(bf16)
        if step < 2:
            edge_ref[step] = pairs.astype(bf16)
            out_copies[step].start()
    for copy in out_copies:
        copy.wait()


def in_hbm(*arrays):
    return [pltpu.with_memory_space_constraint(array, pltpu.HBM) for array in arrays]


def fine_project(place, x, gain, weight):
    vmem, hbm = pl.BlockSpec(memory_space=pltpu.VMEM), pl.BlockSpec(memory_space=pltpu.HBM)
    return pl.pallas_call(
        fine_project_kernel,
        in_specs=[pl.BlockSpec(memory_space=pltpu.SMEM), hbm, hbm, hbm],
        out_specs=[vmem, vmem, vmem, hbm, hbm, hbm, hbm],
        out_shape=[
            jax.ShapeDtypeStruct((4, TOKENS, 192), bf16),
            jax.ShapeDtypeStruct((4, 192, TOKENS), bf16),
            jax.ShapeDtypeStruct((4, TOKENS, 256), bf16),
            pltpu.HBM((TOKENS, 384), bf16),
            pltpu.HBM((TOKENS, 384), bf16),
            pltpu.HBM((32, 768), f32),
            pltpu.HBM((4, TOKENS, 192), bf16),
        ],
        scratch_shapes=[
            pltpu.VMEM((4, TOKENS, 768), bf16),
            pltpu.VMEM((768,), f32),
            pltpu.VMEM((3, 192, 768), bf16),
            pltpu.VMEM((576, 768), bf16),
            pltpu.VMEM((128, 768), f32),
            pltpu.VMEM((2, TOKENS, 384), bf16),
            pltpu.VMEM((4, TOKENS, 192), bf16),
            pltpu.VMEM((32, 768), f32),
            pltpu.SemaphoreType.DMA((6,)),
            pltpu.SemaphoreType.DMA((4,)),
        ],
        compiler_params=params(24),
        cost_estimate=cost(2 * 2048 * 768 * 768, 8e6),
        name="fine_project",
    )(place, *in_hbm(x, gain, weight))


BASES = (0, 0, 128, 128)
WINDOWS = ((0, 256), (0, 384), (128, 512), (256, 512))


def near_keys(tile, base):
    query = lax.broadcasted_iota(jnp.int32, (128, 384), 0) + 128 * tile
    key = lax.broadcasted_iota(jnp.int32, (128, 384), 1) + base
    rows = jnp.abs((query >> 5) - (key >> 5))
    cols = jnp.abs((query & 31) - (key & 31))
    return (rows <= REACH) & (cols <= REACH)


def outside_range(total, least):
    low = lax.broadcasted_iota(jnp.int32, (128, 128), 1) < 64
    bad = jnp.where((total < 2.0**60) & (least > 2.0**-60), 0.0, 1.0)
    return jnp.max(jnp.where(low, bad, 0.0))


def rows_at(part, tile):
    start = part * TOKENS + tile * 128
    return pl.ds(start if isinstance(start, int) else pl.multiple_of(start, 128), 128)


def window_of(tile):
    base = pl.multiple_of((tile >> 1) * 128, 128)
    return base, pl.ds(base, 384), pl.ds(pl.multiple_of(tile * 128, 128), 128)


def put_rows(out_ref, tile, pair):
    low = lax.broadcasted_iota(jnp.int32, (128, 128), 1) < 64
    thirds, counts = [], []
    for at, sums in enumerate(pair):
        turned = [pltpu.roll(one, 64, axis=1) for one in sums]
        heads = [one / other for one, other in zip(sums, turned)]
        out_ref[0, rows_at(at, tile), :] = jnp.where(
            low, heads[0], heads[1]
        ).astype(bf16)
        thirds.append(heads[2])
        counts += [turned[0], sums[1], turned[2]]
    packed = jnp.where(low, thirds[0], pltpu.roll(thirds[1], 64, axis=1))
    out_ref[0, rows_at(2, tile), :] = packed.astype(bf16)
    return sum(counts), functools.reduce(jnp.minimum, counts)


def stack_heads(query):
    head = lax.broadcasted_iota(jnp.int32, (1, 192), 1) >> 6
    return jnp.concatenate(
        [query * jnp.where(head == i, 1.0, 0.0).astype(bf16) for i in range(3)], axis=0
    )


def own_parts(summed):
    low = lax.broadcasted_iota(jnp.int32, (1, 128, 128), 2) < 64
    first, second = summed[..., :128], summed[..., 128:]
    n = summed.shape[1]
    turned = pltpu.roll(second[1].reshape(n * 128, 128), 64, axis=1).reshape(n, 128, 128)
    return [
        jnp.where(low, first[0], second[0]),
        jnp.where(low, turned, first[1]),
        second[2],
    ]


def attend_again(q_ref, frames, out_ref):
    def redo(tile, _):
        base, window, own = window_of(tile)
        near = jnp.concatenate([near_keys(tile, base)] * 3, axis=0)
        pair = []
        for frame, sources in frames:
            query = stack_heads(q_ref[frame, own, :])
            scores = []
            for keys, _, inside in sources:
                seen = near if inside is None else near & (inside > 0.0)
                scores.append(jnp.where(seen, nn_dot(query, keys[:, window]), -jnp.inf))
            top = jnp.max(
                jnp.maximum(jnp.maximum(scores[0], scores[1]), scores[2]), axis=-1, keepdims=True
            )
            summed = sum(
                nn_dot(jnp.exp2(score - top).astype(bf16), ones[window, :])
                for score, (_, ones, _) in zip(scores, sources)
            )
            pair.append([part[0] for part in own_parts(summed.reshape(3, 1, 128, 256))])
        put_rows(out_ref, tile, pair)
        return 0

    lax.fori_loop(0, 4, redo, 0)


def weigh(query, keys, ones, mask):
    n = query.shape[0]
    weights = jnp.exp2(nn_dot(stack_heads(query.reshape(n * 128, 192)), keys)).astype(bf16)
    weights = (weights.reshape(3 * n, *mask.shape) * mask[None]).reshape(-1, mask.shape[1])
    return own_parts(nn_dot(weights, ones).reshape(3, n, 128, 256))


def tiles():
    for tile in range(4):
        first, last = WINDOWS[tile]
        own = slice(128 * tile, 128 * tile + 128)
        yield tile, own, slice(first, last), slice(first - BASES[tile], last - BASES[tile])


def block_means(out_ref):
    matrix = block_mean_matrix(ROWS).astype(bf16)
    pairs = nn_dot(matrix, out_ref[0, :TOKENS, :])
    pairs += nn_dot(matrix, out_ref[0, TOKENS : 2 * TOKENS, :])
    return pairs, nn_dot(matrix, out_ref[0, 2 * TOKENS :, :])


def set_weights(weight_ref, first_ref, third_ref):
    first_ref[...] = jnp.zeros_like(first_ref)
    third_ref[...] = jnp.zeros_like(third_ref)
    for place in range(4):
        weight = weight_ref[:, 192 * place : 192 * place + 192]
        lanes = slice(128 * place, 128 * place + 128)
        for at in (0, 1):
            first_ref[at, :128, lanes] = weight[:128, :128]
            first_ref[at, 128 + 64 * at : 192 + 64 * at, lanes] = weight[128:, :128]
            half = slice(128 * place + 64 * at, 128 * place + 64 * at + 64)
            third_ref[128 * at : 128 * at + 128, half] = weight[:128, 128:]
            third_ref[256 + 64 * at : 320 + 64 * at, half] = weight[128:, 128:]


def put_products(rows_ref, first_ref, third_ref, out_ref, out_hbm, sems):
    parts = [rows_ref[0, TOKENS * i : TOKENS * (i + 1), :] for i in range(3)]
    copies = []
    for i in range(3):
        if i < 2:
            product = nn_dot(jnp.concatenate([parts[i], parts[2]], axis=1), first_ref[i])
        else:
            product = nn_dot(jnp.concatenate(parts, axis=1), third_ref[...])
        own = pl.ds(TOKENS * i, TOKENS)
        for place in range(4):
            out_ref[place, own, :] = product[:, 128 * place : 128 * place + 128].astype(bf16)
        copies.append(
            pltpu.make_async_copy(out_ref.at[:, own, :], out_hbm.at[:, own, :], sems.at[i])
        )
        copies[-1].start()
    for copy in copies:
        copy.wait()


def inner_kernel(
    q_ref, k_ref, v_ref, weight_hbm,
    out_hbm, mask_ref, mean_ref, part_ref, first_ref, third_ref, rows_ref, out_ref, weight_ref, sems,
):
    weight_copy = pltpu.make_async_copy(weight_hbm, weight_ref, sems.at[3])
    weight_copy.start()

    total, least = jnp.zeros((128, 128), f32), jnp.ones((128, 128), f32)
    for tile, own, window, seen in tiles():
        mask_ref[tile] = jnp.where(near_keys(tile, BASES[tile]), 1.0, 0.0).astype(bf16)
        sums = [None] * 4
        for g in range(4):
            lo, hi = max(g - 1, 0), min(g + 1, 3)
            parts = weigh(
                q_ref[lo : hi + 1, own, :],
                k_ref[g, :, window],
                v_ref[g, window, :],
                mask_ref[tile, :, seen],
            )
            for f in range(lo, hi + 1):
                here = [part[f - lo] for part in parts]
                sums[f] = here if sums[f] is None else [a + b for a, b in zip(sums[f], here)]
        for head in range(3):
            lanes = slice(128 * head, 128 * head + 128)
            part_ref[0, own, lanes] = sums[0][head]
            part_ref[1, own, lanes] = sums[3][head]
        tile_total, tile_least = put_rows(rows_ref, tile, sums[1:3])
        total, least = total + tile_total, jnp.minimum(least, tile_least)
    bad = outside_range(total, least)

    @pl.when(bad > 0.0)
    def _():
        own_frames = [(k_ref.at[g], v_ref.at[g], None) for g in range(4)]
        attend_again(q_ref, [(1, own_frames[:3]), (2, own_frames[1:])], rows_ref)

    mean_ref[:, :128], mean_ref[:, 128:] = block_means(rows_ref)
    weight_copy.wait()
    set_weights(weight_ref, first_ref, third_ref)
    put_products(rows_ref, first_ref, third_ref, out_ref, out_hbm.at[:, 0], sems)


def outer_kernel(
    edge_ref, mask_ref, q_ref, k_ref, v_ref, part_ref, halo_first_ref, halo_last_ref,
    inner_mean_ref, first_ref, third_ref, weight_hbm, inner_ref,
    out_hbm, partial_ref, halo_key_ref, halo_ones_ref,
    rows_ref, out_ref, weight_ref, sems,
):
    weight_copy = pltpu.make_async_copy(weight_hbm, weight_ref, sems.at[3])
    weight_copy.start()
    lane = lax.broadcasted_iota(jnp.int32, (1, 256), 1)
    for at, halo_ref in enumerate((halo_first_ref, halo_last_ref)):
        halo = halo_ref[...].astype(f32)
        halo_ones_ref[at] = (jnp.where(lane < 192, halo[:, :256], 1.0) * edge_ref[at]).astype(bf16)
        halo_key_ref[at] = jnp.transpose(halo)[192:].astype(bf16)

    total, least = jnp.zeros((128, 128), f32), jnp.ones((128, 128), f32)
    for tile, own, window, seen in tiles():
        pair = []
        for at, frame in enumerate((0, 3)):
            more = weigh(
                q_ref[frame : frame + 1, own, :],
                halo_key_ref[at, :, window],
                halo_ones_ref[at, window, :],
                mask_ref[tile, :, seen],
            )
            pair.append(
                [
                    part_ref[at, own, 128 * head : 128 * head + 128] + more[head][0]
                    for head in range(3)
                ]
            )
        tile_total, tile_least = put_rows(rows_ref, tile, pair)
        total, least = total + tile_total, jnp.minimum(least, tile_least)
    bad = outside_range(total, least)

    @pl.when(bad > 0.0)
    def _():
        own_frames = [(k_ref.at[g], v_ref.at[g], None) for g in range(4)]
        halos = [(halo_key_ref.at[at], halo_ones_ref.at[at], edge_ref[at]) for at in (0, 1)]
        attend_again(
            q_ref, [(0, own_frames[:2] + halos[:1]), (3, own_frames[2:] + halos[1:])], rows_ref
        )

    here = block_means(rows_ref)
    pairs = here[0] + inner_mean_ref[:, :128]
    third = here[1] + inner_mean_ref[:, 128:]
    third = third + pltpu.roll(third, 64, axis=1)
    weight_copy.wait()
    partial = nn_dot(pairs.astype(bf16), weight_ref[:128, :])
    partial += nn_dot(third[:, :64].astype(bf16), weight_ref[128:, :])
    partial_ref[...] = partial.astype(bf16)
    put_products(rows_ref, first_ref, third_ref, out_ref, out_hbm.at[:, 1], sems)


OUT_SCRATCH = [
    pltpu.VMEM((1, 3 * TOKENS, 128), bf16),
    pltpu.VMEM((4, 3 * TOKENS, 128), bf16),
    pltpu.VMEM((192, 768), bf16),
    pltpu.SemaphoreType.DMA((4,)),
]


def attend_inner(q, k, v, weight):
    vmem, hbm = pl.BlockSpec(memory_space=pltpu.VMEM), pl.BlockSpec(memory_space=pltpu.HBM)
    return pl.pallas_call(
        inner_kernel,
        in_specs=[vmem] * 3 + [hbm],
        out_specs=[hbm] + [vmem] * 5,
        out_shape=[
            pltpu.HBM((4, 2, 3 * TOKENS, 128), bf16),
            jax.ShapeDtypeStruct((4, 128, 384), bf16),
            jax.ShapeDtypeStruct((32, 256), f32),
            jax.ShapeDtypeStruct((2, TOKENS, 384), f32),
            jax.ShapeDtypeStruct((2, 256, 512), bf16),
            jax.ShapeDtypeStruct((384, 512), bf16),
        ],
        scratch_shapes=OUT_SCRATCH,
        compiler_params=params(24),
        cost_estimate=cost(10 * 2 * 512 * 320 * 3 * 256, 6e6, 10 * 512 * 320 * 3),
        name="attend_inner",
    )(q, k, v, *in_hbm(weight))


def attend_outer(
    edge, mask, q, k, v, part, first, last, inner_mean, weight, first_weight, third_weight, inner
):
    vmem, hbm = pl.BlockSpec(memory_space=pltpu.VMEM), pl.BlockSpec(memory_space=pltpu.HBM)
    return pl.pallas_call(
        outer_kernel,
        in_specs=[pl.BlockSpec(memory_space=pltpu.SMEM)] + [vmem] * 10 + [hbm] * 2,
        out_specs=[hbm, vmem],
        out_shape=[
            pltpu.HBM((4, 2, 3 * TOKENS, 128), bf16),
            jax.ShapeDtypeStruct((32, 768), bf16),
        ],
        input_output_aliases={12: 0},
        scratch_shapes=[
            pltpu.VMEM((2, 192, TOKENS), bf16),
            pltpu.VMEM((2, TOKENS, 256), bf16),
        ]
        + OUT_SCRATCH,
        compiler_params=params(24),
        cost_estimate=cost(2 * 2 * 512 * 320 * 3 * 256, 6e6, 2 * 512 * 320 * 3),
        name="attend_outer",
    )(
        edge, mask, q, k, v, part, first, last, inner_mean, first_weight, third_weight,
        *in_hbm(weight), inner,
    )


def load_kernel(_, *refs):
    sources, targets, sems = refs[:4], refs[4:8], refs[8]
    copies = [
        pltpu.make_async_copy(source, target, sems.at[i])
        for i, (source, target) in enumerate(zip(sources, targets))
    ]
    for copy in copies:
        copy.start()
    for copy in copies:
        copy.wait()


def load(after, *arrays):
    anywhere = pl.BlockSpec(memory_space=pl.ANY)
    return pl.pallas_call(
        load_kernel,
        in_specs=[anywhere] * 5,
        out_specs=[anywhere] * 4,
        out_shape=[pltpu.VMEM(array.shape, array.dtype) for array in arrays],
        scratch_shapes=[pltpu.SemaphoreType.DMA((4,))],
        compiler_params=params(4),
        cost_estimate=cost(0, 6e6),
        name="load",
    )(after, *in_hbm(*arrays))


def coarse_project_kernel(
    p0, p1, p2, p3, mean_ref, merge_ref, gain_ref, weight_ref, coarse_ref, q_ref, kv_ref
):
    pooled = mean_ref[...] + (
        (p0[...].astype(f32) + p1[...].astype(f32)) + (p2[...].astype(f32) + p3[...].astype(f32))
    )
    coarse = nn_dot(pooled.astype(bf16), merge_ref[...]).astype(bf16)
    coarse_ref[...] = coarse
    wide = coarse.astype(f32)
    scale = lax.rsqrt(jnp.mean(wide * wide, axis=-1, keepdims=True) + EPSILON)
    normed = (wide * scale * gain_ref[...].reshape(1, 1536)).astype(bf16)
    q_ref[...] = (nn_dot(normed, weight_ref[0]) * (128**-0.5 * LOG2E)).astype(bf16)
    key = nn_dot(normed, weight_ref[1]).astype(bf16)
    value = nn_dot(normed, weight_ref[2]).astype(bf16)
    for copy in range(8):
        kv_ref[copy, :, :384] = key
        kv_ref[copy, :, 384:] = value


def coarse_project(partials, mean, merge, gain, weight):
    return pl.pallas_call(
        coarse_project_kernel,
        in_specs=[pl.BlockSpec(memory_space=pltpu.VMEM)] * 8,
        out_specs=[whole(32, 1536), whole(32, 384), whole(8, 32, 768)],
        out_shape=[
            jax.ShapeDtypeStruct((32, 1536), bf16),
            jax.ShapeDtypeStruct((32, 384), bf16),
            pltpu.HBM((8, 32, 768), bf16),
        ],
        compiler_params=params(20),
        cost_estimate=cost(2 * 32 * 1536 * 1920, 7e6),
        name="coarse_project",
    )(*partials, mean, merge, gain, weight)


def coarse_attend_kernel(
    q0, q1, q2, q3, kv_ref, other_ref, split_hbm, o0, o1, o2, o3, split_out, sems
):
    split_copy = pltpu.make_async_copy(split_hbm, split_out, sems.at[0])
    split_copy.start()
    query = jnp.concatenate([ref[...] for ref in (q0, q1, q2, q3)], axis=0)
    outs = (o0, o1, o2, o3)
    lane = lax.broadcasted_iota(jnp.int32, (128, 128), 1)
    stats = jnp.zeros((128, 128), f32)
    for head in range(3):
        lanes = slice(128 * head, 128 * head + 128)
        values = slice(384 + 128 * head, 512 + 128 * head)
        scores = [nt_dot(query[:, lanes], ref[:, lanes]) for ref in (kv_ref, other_ref)]
        top = jnp.max(jnp.maximum(scores[0], scores[1]), axis=-1, keepdims=True)
        weights = [jnp.exp2(score - top) for score in scores]
        total = jnp.sum(weights[0] + weights[1], axis=-1, keepdims=True)
        summed = nn_dot(weights[0].astype(bf16), kv_ref[:, values])
        summed += nn_dot(weights[1].astype(bf16), other_ref[:, values])
        summed = (summed / total).astype(bf16)
        rest = top + jnp.log(total) * LOG2E
        for part in range(3):
            piece = rest.astype(bf16).astype(f32)
            stats = jnp.where(lane == 3 * head + part, piece, stats)
            rest = rest - piece
        for i, out in enumerate(outs):
            out[:, lanes] = summed[32 * i : 32 * i + 32]
    for i, out in enumerate(outs):
        out[:, 384:] = stats[32 * i : 32 * i + 32].astype(bf16)
    split_copy.wait()


def coarse_attend(queries, kv, other, split):
    vmem, anywhere = pl.BlockSpec(memory_space=pltpu.VMEM), pl.BlockSpec(memory_space=pl.ANY)
    return pl.pallas_call(
        coarse_attend_kernel,
        in_specs=[vmem] * 6 + [anywhere],
        out_specs=[vmem] * 4 + [anywhere],
        out_shape=[jax.ShapeDtypeStruct((32, 512), bf16)] * 4 + [pltpu.VMEM(split.shape, bf16)],
        scratch_shapes=[pltpu.SemaphoreType.DMA((1,))],
        compiler_params=params(16),
        cost_estimate=cost(4 * 128 * 512 * 384, 1e6, 128 * 512 * 3),
        name="coarse_attend",
    )(*queries, kv, other, *in_hbm(split))


def coarse_combine_kernel(p0, p1, p2, p3, weight_ref, out_ref):
    parts = (p0, p1, p2, p3)
    heads = []
    for head in range(3):
        lanes = slice(128 * head, 128 * head + 128)
        logs = [
            jnp.sum(part[:, 384 + 3 * head : 387 + 3 * head].astype(f32), axis=-1, keepdims=True)
            for part in parts
        ]
        top = functools.reduce(jnp.maximum, logs)
        shares = [jnp.exp2(log - top) for log in logs]
        summed = sum(share * part[:, lanes].astype(f32) for share, part in zip(shares, parts))
        heads.append((summed / sum(shares)).astype(bf16))
    attended = jnp.concatenate(heads, axis=-1)
    out_ref[...] = nn_dot(attended, weight_ref[...]).astype(bf16)


def coarse_combine(parts, weight):
    return pl.pallas_call(
        coarse_combine_kernel,
        out_shape=jax.ShapeDtypeStruct((32, 1536), bf16),
        compiler_params=params(16),
        cost_estimate=cost(2 * 32 * 384 * 1536, 2e6),
        name="coarse_combine",
    )(*parts, weight)


def split_kernel(
    x_hbm, rows_hbm, coarse_ref, p0, p1, p2, p3, weight_ref, out_hbm,
    x_ref, rows_ref, out_ref, in_sems, out_sems,
):
    x_copy = pltpu.make_async_copy(x_hbm, x_ref, in_sems.at[2])
    x_copy.start()
    in_copies = [
        pltpu.make_async_copy(rows_hbm.at[pair], rows_ref.at[pair], in_sems.at[pair])
        for pair in (0, 1)
    ]
    for copy in in_copies:
        copy.start()
    mixed = (p0[...].astype(f32) + p1[...].astype(f32)) + (
        p2[...].astype(f32) + p3[...].astype(f32)
    )
    after = (coarse_ref[...].astype(f32) + mixed).astype(bf16)
    split = nt_dot(after, weight_ref[...])
    row = lax.broadcasted_iota(jnp.int32, (128, 32), 0)
    col = lax.broadcasted_iota(jnp.int32, (128, 32), 1)
    spread = jnp.where(col == (row >> 5) * 8 + ((row & 31) >> 2), 1.0, 0.0)
    grid = jnp.dot(spread, split, preferred_element_type=f32, precision=lax.Precision.HIGHEST)
    out_copies = []
    x_copy.wait()
    for pair, frames in enumerate(((1, 2), (0, 3))):
        in_copies[pair].wait()
        third = rows_ref[pair, 2 * TOKENS :, :].astype(f32)
        for at, frame in enumerate(frames):
            x = x_ref[frame].astype(f32)
            one = rows_ref[pair, TOKENS * at : TOKENS * (at + 1), :].astype(f32)
            two = pltpu.roll(third, 64, axis=1) if at else third
            for lanes, added in ((slice(0, 128), one), (slice(128, 192), two[:, :64])):
                hidden = (x[:, lanes] + added).astype(bf16).astype(f32)
                hidden = hidden.reshape(4, 4, COLS, -1) + grid[:, lanes].reshape(4, 1, COLS, -1)
                out_ref[frame, :, :, lanes] = hidden.reshape(ROWS, COLS, -1).astype(bf16)
            out_copies.append(
                pltpu.make_async_copy(out_ref.at[frame], out_hbm.at[frame], out_sems.at[frame])
            )
            out_copies[-1].start()
    for copy in out_copies:
        copy.wait()


def split_rows(x, rows, coarse, partials, weight):
    vmem, hbm = pl.BlockSpec(memory_space=pltpu.VMEM), pl.BlockSpec(memory_space=pltpu.HBM)
    return pl.pallas_call(
        split_kernel,
        in_specs=[hbm, hbm] + [vmem] * 6,
        out_specs=hbm,
        out_shape=jax.ShapeDtypeStruct((4, ROWS, COLS, 192), bf16),
        scratch_shapes=[
            pltpu.VMEM((4, TOKENS, 192), bf16),
            pltpu.VMEM((2, 3 * TOKENS, 128), bf16),
            pltpu.VMEM((4, ROWS, COLS, 192), bf16),
            pltpu.SemaphoreType.DMA((3,)),
            pltpu.SemaphoreType.DMA((4,)),
        ],
        compiler_params=params(24),
        cost_estimate=cost(2 * 32 * 1536 * 192, 4e6),
        name="split_rows",
    )(*in_hbm(x, rows), coarse, *partials, weight)


def shifted(value, axis, shift):
    return lax.ppermute(value, axis, [(i, (i + shift) % 4) for i in range(4)])


def from_others(value, axis):
    return [shifted(value, axis, shift) for shift in (1, 2, 3)]


def body(x, fine_gain, fine_qkv, fine_out, merge, coarse_gain, coarse_qkv, coarse_out, split):
    x = x.reshape(4, TOKENS, 768)
    groups = lax.axis_size(FRAMES)
    here = lax.axis_index(FRAMES)
    place = lax.axis_index("mp").astype(jnp.int32).reshape(1)
    edge = jnp.stack(
        [jnp.where(here == 0, 0.0, 1.0), jnp.where(here == groups - 1, 0.0, 1.0)]
    ).astype(f32)

    q, k, v, initial, final, frame_mean, own = fine_project(
        place, x, fine_gain, jnp.transpose(fine_qkv, (1, 2, 0))
    )
    first = lax.ppermute(final, FRAMES, [(i, i + 1) for i in range(groups - 1)])
    last = lax.ppermute(initial, FRAMES, [(i + 1, i) for i in range(groups - 1)])
    inner, mask, inner_mean, part, *weights = attend_inner(q, k, v, fine_out)
    products, partial = attend_outer(
        edge, mask, q, k, v, part, first, last, inner_mean, fine_out, *weights, inner
    )
    partials = from_others(partial, "mp")
    rows = lax.psum_scatter(products, "mp", scatter_dimension=0, tiled=True)
    frame_mean, merge, coarse_qkv, coarse_gain = load(
        partials[0], frame_mean, merge, jnp.transpose(coarse_qkv, (1, 0, 2)), coarse_gain
    )

    coarse, coarse_q, coarse_kv = coarse_project(
        [partial] + partials, frame_mean, merge, coarse_gain, coarse_qkv
    )
    coarse_kv = lax.all_to_all(coarse_kv, "z", 0, 0, tiled=True).reshape(256, 768)
    queries = [coarse_q] + from_others(coarse_q, "x")
    coarse_kv, queries = lax.optimization_barrier((coarse_kv, queries))
    other_kv = lax.ppermute(coarse_kv, "core", [(0, 1), (1, 0)])
    *parts, split = coarse_attend(queries, coarse_kv, other_kv, jnp.transpose(split, (1, 0)))
    parts = parts[:1] + [shifted(parts[s], "x", 4 - s) for s in (1, 2, 3)]
    coarse_partial = coarse_combine(parts, coarse_out)
    coarse_partials = [coarse_partial] + from_others(coarse_partial, "mp")
    return split_rows(
        own, rows.reshape(2, 3 * TOKENS, 128), coarse, coarse_partials, split
    )


def solution(mesh):
    parts = jax.sharding.Mesh(mesh.devices.reshape(4, 8, 2, 4), FRAMES + ("mp",))
    in_specs = (
        P(FRAMES, None, None, None),
        P(),
        P(None, None, "mp"),
        P("mp", None),
        P(),
        P(),
        P(None, None, "mp"),
        P("mp", None),
        P(None, "mp"),
    )
    out_specs = P(FRAMES, None, None, "mp")
    return jax.shard_map(body, mesh=parts, in_specs=in_specs, out_specs=out_specs, check_vma=False)
```

```python
import functools

import jax
import jax.numpy as jnp
from jax import lax
from jax.experimental import pallas as pl
from jax.experimental.pallas import tpu as pltpu
from jax.sharding import PartitionSpec as P

HEADS = 12
EPSILON = 1e-06
REACH = 3
LOG2E = 1.4426950408889634
ROWS, COLS = 16, 32
TOKENS = ROWS * COLS
FRAMES = ("x", "z", "core")
MIB = 1 << 20
bf16, f32 = jnp.bfloat16, jnp.float32


def nt_dot(a, b):
    return lax.dot_general(a, b, (((1,), (1,)), ((), ())), preferred_element_type=f32)


def nn_dot(a, b):
    return jnp.dot(a, b, preferred_element_type=f32)


def block_mean_matrix(rows):
    token = lax.broadcasted_iota(jnp.int32, (32, rows * COLS), 1)
    block = lax.broadcasted_iota(jnp.int32, (32, rows * COLS), 0)
    of_token = token // (rows * COLS // 4) * 8 + ((token & 31) >> 2)
    return jnp.where(of_token == block, 1.0 / 64, 0.0)


def params(mib):
    return pltpu.CompilerParams(vmem_limit_bytes=mib * MIB)


def cost(flops, bytes_accessed, transcendentals=0):
    return pl.CostEstimate(
        flops=int(flops), bytes_accessed=int(bytes_accessed), transcendentals=int(transcendentals)
    )


def whole(*shape):
    return pl.BlockSpec(shape, lambda *i: (0,) * len(shape))


def fine_project_kernel(
    place_ref, x_hbm, gain_hbm, weight_hbm,
    q_ref, key_ref, ones_ref, initial_hbm, last_hbm, mean_hbm, own_hbm,
    x_ref, gain_ref, weight_ref, rows_ref, sum_ref, edge_ref, own_ref, mean_ref,
    in_sems, out_sems,
):
    gain_copy = pltpu.make_async_copy(gain_hbm, gain_ref, in_sems.at[5])
    gain_copy.start()
    weight_copy = pltpu.make_async_copy(weight_hbm, weight_ref, in_sems.at[4])
    weight_copy.start()
    x_copies = [
        pltpu.make_async_copy(x_hbm.at[frame], x_ref.at[frame], in_sems.at[frame])
        for frame in range(4)
    ]
    order = (0, 3, 1, 2)
    for frame in order:
        x_copies[frame].start()
    gain_copy.wait()
    weight_copy.wait()
    gain = gain_ref[...].reshape(1, 768)
    query, key, value = (weight_ref[i].astype(f32) * gain for i in range(3))
    rows_ref[:192, :] = value.astype(bf16)
    rows_ref[192:384, :] = key.astype(bf16)
    rows_ref[384:, :] = (query * (0.125 * LOG2E)).astype(bf16)

    out_copies = [
        pltpu.make_async_copy(edge_ref.at[i], out, out_sems.at[i])
        for i, out in enumerate((initial_hbm, last_hbm))
    ]

    for step, frame in enumerate(order):
        x_copies[frame].wait()
        if step == 3:
            for place in range(4):

                @pl.when(place_ref[0] == place)
                def _():
                    own_ref[...] = x_ref[:, :, 192 * place : 192 * place + 192]

            out_copies.append(pltpu.make_async_copy(own_ref, own_hbm, out_sems.at[2]))
            out_copies[-1].start()
        x = x_ref[frame]
        wide = x.astype(f32)
        added = jnp.sum(wide.reshape(4, 4, COLS, 768), axis=1).reshape(4 * COLS, 768)
        sum_ref[...] = sum_ref[...] + added if step else added
        if step == 3:
            mean_ref[...] = jnp.dot(
                block_mean_matrix(4),
                sum_ref[...],
                preferred_element_type=f32,
                precision=lax.Precision.HIGHEST,
            )
            out_copies.append(pltpu.make_async_copy(mean_ref, mean_hbm, out_sems.at[3]))
            out_copies[-1].start()
        projected = nt_dot(x, rows_ref[...])
        scale = lax.rsqrt(jnp.mean(wide * wide, axis=-1, keepdims=True) + EPSILON)
        projected = projected * scale
        q_ref[frame] = projected[:, 384:].astype(bf16)
        pairs = projected[:, :384]
        lane = lax.broadcasted_iota(jnp.int32, (1, 256), 1)
        ones_ref[frame] = jnp.where(lane < 192, projected[:, :256], 1.0).astype(bf16)
        along = jnp.transpose(jnp.broadcast_to(scale, (TOKENS, 128)))[:1]
        key_ref[frame] = (nt_dot(rows_ref[192:384, :], x) * along).astype(bf16)
        if step < 2:
            edge_ref[step] = pairs.astype(bf16)
            out_copies[step].start()
    for copy in out_copies:
        copy.wait()


def in_hbm(*arrays):
    return [pltpu.with_memory_space_constraint(array, pltpu.HBM) for array in arrays]


def fine_project(place, x, gain, weight):
    vmem, hbm = pl.BlockSpec(memory_space=pltpu.VMEM), pl.BlockSpec(memory_space=pltpu.HBM)
    return pl.pallas_call(
        fine_project_kernel,
        in_specs=[pl.BlockSpec(memory_space=pltpu.SMEM), hbm, hbm, hbm],
        out_specs=[vmem, vmem, vmem, hbm, hbm, hbm, hbm],
        out_shape=[
            jax.ShapeDtypeStruct((4, TOKENS, 192), bf16),
            jax.ShapeDtypeStruct((4, 192, TOKENS), bf16),
            jax.ShapeDtypeStruct((4, TOKENS, 256), bf16),
            pltpu.HBM((TOKENS, 384), bf16),
            pltpu.HBM((TOKENS, 384), bf16),
            pltpu.HBM((32, 768), f32),
            pltpu.HBM((4, TOKENS, 192), bf16),
        ],
        scratch_shapes=[
            pltpu.VMEM((4, TOKENS, 768), bf16),
            pltpu.VMEM((768,), f32),
            pltpu.VMEM((3, 192, 768), bf16),
            pltpu.VMEM((576, 768), bf16),
            pltpu.VMEM((128, 768), f32),
            pltpu.VMEM((2, TOKENS, 384), bf16),
            pltpu.VMEM((4, TOKENS, 192), bf16),
            pltpu.VMEM((32, 768), f32),
            pltpu.SemaphoreType.DMA((6,)),
            pltpu.SemaphoreType.DMA((4,)),
        ],
        compiler_params=params(24),
        cost_estimate=cost(2 * 2048 * 768 * 768, 8e6),
        name="fine_project",
    )(place, *in_hbm(x, gain, weight))


BASES = (0, 0, 128, 128)
WINDOWS = ((0, 256), (0, 384), (128, 512), (256, 512))


def near_keys(tile, base):
    query = lax.broadcasted_iota(jnp.int32, (128, 384), 0) + 128 * tile
    key = lax.broadcasted_iota(jnp.int32, (128, 384), 1) + base
    rows = jnp.abs((query >> 5) - (key >> 5))
    cols = jnp.abs((query & 31) - (key & 31))
    return (rows <= REACH) & (cols <= REACH)


def outside_range(total, least):
    low = lax.broadcasted_iota(jnp.int32, (128, 128), 1) < 64
    bad = jnp.where((total < 2.0**60) & (least > 2.0**-60), 0.0, 1.0)
    return jnp.max(jnp.where(low, bad, 0.0))


def rows_at(part, tile):
    start = part * TOKENS + tile * 128
    return pl.ds(start if isinstance(start, int) else pl.multiple_of(start, 128), 128)


def window_of(tile):
    base = pl.multiple_of((tile >> 1) * 128, 128)
    return base, pl.ds(base, 384), pl.ds(pl.multiple_of(tile * 128, 128), 128)


def put_rows(out_ref, tile, pair):
    low = lax.broadcasted_iota(jnp.int32, (128, 128), 1) < 64
    thirds, counts = [], []
    for at, sums in enumerate(pair):
        turned = [pltpu.roll(one, 64, axis=1) for one in sums]
        heads = [one / other for one, other in zip(sums, turned)]
        out_ref[0, rows_at(at, tile), :] = jnp.where(
            low, heads[0], heads[1]
        ).astype(bf16)
        thirds.append(heads[2])
        counts += [turned[0], sums[1], turned[2]]
    packed = jnp.where(low, thirds[0], pltpu.roll(thirds[1], 64, axis=1))
    out_ref[0, rows_at(2, tile), :] = packed.astype(bf16)
    return sum(counts), functools.reduce(jnp.minimum, counts)


def stack_heads(query):
    head = lax.broadcasted_iota(jnp.int32, (1, 192), 1) >> 6
    return jnp.concatenate(
        [query * jnp.where(head == i, 1.0, 0.0).astype(bf16) for i in range(3)], axis=0
    )


def own_parts(summed):
    low = lax.broadcasted_iota(jnp.int32, (1, 128, 128), 2) < 64
    first, second = summed[..., :128], summed[..., 128:]
    n = summed.shape[1]
    turned = pltpu.roll(second[1].reshape(n * 128, 128), 64, axis=1).reshape(n, 128, 128)
    return [
        jnp.where(low, first[0], second[0]),
        jnp.where(low, turned, first[1]),
        second[2],
    ]


def attend_again(q_ref, frames, out_ref):
    def redo(tile, _):
        base, window, own = window_of(tile)
        near = jnp.concatenate([near_keys(tile, base)] * 3, axis=0)
        pair = []
        for frame, sources in frames:
            query = stack_heads(q_ref[frame, own, :])
            scores = []
            for keys, _, inside in sources:
                seen = near if inside is None else near & (inside > 0.0)
                scores.append(jnp.where(seen, nn_dot(query, keys[:, window]), -jnp.inf))
            top = jnp.max(
                jnp.maximum(jnp.maximum(scores[0], scores[1]), scores[2]), axis=-1, keepdims=True
            )
            summed = sum(
                nn_dot(jnp.exp2(score - top).astype(bf16), ones[window, :])
                for score, (_, ones, _) in zip(scores, sources)
            )
            pair.append([part[0] for part in own_parts(summed.reshape(3, 1, 128, 256))])
        put_rows(out_ref, tile, pair)
        return 0

    lax.fori_loop(0, 4, redo, 0)


def weigh(query, keys, ones, mask):
    n = query.shape[0]
    weights = jnp.exp2(nn_dot(stack_heads(query.reshape(n * 128, 192)), keys)).astype(bf16)
    weights = (weights.reshape(3 * n, *mask.shape) * mask[None]).reshape(-1, mask.shape[1])
    return own_parts(nn_dot(weights, ones).reshape(3, n, 128, 256))


def tiles():
    for tile in range(4):
        first, last = WINDOWS[tile]
        own = slice(128 * tile, 128 * tile + 128)
        yield tile, own, slice(first, last), slice(first - BASES[tile], last - BASES[tile])


def block_means(out_ref):
    matrix = block_mean_matrix(ROWS).astype(bf16)
    pairs = nn_dot(matrix, out_ref[0, :TOKENS, :])
    pairs += nn_dot(matrix, out_ref[0, TOKENS : 2 * TOKENS, :])
    return pairs, nn_dot(matrix, out_ref[0, 2 * TOKENS :, :])


def set_weights(weight_ref, first_ref, third_ref):
    first_ref[...] = jnp.zeros_like(first_ref)
    third_ref[...] = jnp.zeros_like(third_ref)
    for place in range(4):
        weight = weight_ref[:, 192 * place : 192 * place + 192]
        lanes = slice(128 * place, 128 * place + 128)
        for at in (0, 1):
            first_ref[at, :128, lanes] = weight[:128, :128]
            first_ref[at, 128 + 64 * at : 192 + 64 * at, lanes] = weight[128:, :128]
            half = slice(128 * place + 64 * at, 128 * place + 64 * at + 64)
            third_ref[128 * at : 128 * at + 128, half] = weight[:128, 128:]
            third_ref[256 + 64 * at : 320 + 64 * at, half] = weight[128:, 128:]


def put_products(rows_ref, first_ref, third_ref, out_ref, out_hbm, sems):
    parts = [rows_ref[0, TOKENS * i : TOKENS * (i + 1), :] for i in range(3)]
    copies = []
    for i in range(3):
        if i < 2:
            product = nn_dot(jnp.concatenate([parts[i], parts[2]], axis=1), first_ref[i])
        else:
            product = nn_dot(jnp.concatenate(parts, axis=1), third_ref[...])
        own = pl.ds(TOKENS * i, TOKENS)
        for place in range(4):
            out_ref[place, own, :] = product[:, 128 * place : 128 * place + 128].astype(bf16)
        copies.append(
            pltpu.make_async_copy(out_ref.at[:, own, :], out_hbm.at[:, own, :], sems.at[i])
        )
        copies[-1].start()
    for copy in copies:
        copy.wait()


def inner_kernel(
    q_ref, k_ref, v_ref, weight_hbm,
    out_hbm, mask_ref, mean_ref, part_ref, first_ref, third_ref, rows_ref, out_ref, weight_ref, sems,
):
    weight_copy = pltpu.make_async_copy(weight_hbm, weight_ref, sems.at[3])
    weight_copy.start()

    total, least = jnp.zeros((128, 128), f32), jnp.ones((128, 128), f32)
    for tile, own, window, seen in tiles():
        mask_ref[tile] = jnp.where(near_keys(tile, BASES[tile]), 1.0, 0.0).astype(bf16)
        sums = [None] * 4
        for g in range(4):
            lo, hi = max(g - 1, 0), min(g + 1, 3)
            parts = weigh(
                q_ref[lo : hi + 1, own, :],
                k_ref[g, :, window],
                v_ref[g, window, :],
                mask_ref[tile, :, seen],
            )
            for f in range(lo, hi + 1):
                here = [part[f - lo] for part in parts]
                sums[f] = here if sums[f] is None else [a + b for a, b in zip(sums[f], here)]
        for head in range(3):
            lanes = slice(128 * head, 128 * head + 128)
            part_ref[0, own, lanes] = sums[0][head]
            part_ref[1, own, lanes] = sums[3][head]
        tile_total, tile_least = put_rows(rows_ref, tile, sums[1:3])
        total, least = total + tile_total, jnp.minimum(least, tile_least)
    bad = outside_range(total, least)

    @pl.when(bad > 0.0)
    def _():
        own_frames = [(k_ref.at[g], v_ref.at[g], None) for g in range(4)]
        attend_again(q_ref, [(1, own_frames[:3]), (2, own_frames[1:])], rows_ref)

    mean_ref[:, :128], mean_ref[:, 128:] = block_means(rows_ref)
    weight_copy.wait()
    set_weights(weight_ref, first_ref, third_ref)
    put_products(rows_ref, first_ref, third_ref, out_ref, out_hbm.at[:, 0], sems)


def outer_kernel(
    edge_ref, mask_ref, q_ref, k_ref, v_ref, part_ref, halo_first_ref, halo_last_ref,
    inner_mean_ref, first_ref, third_ref, weight_hbm, inner_ref,
    out_hbm, partial_ref, halo_key_ref, halo_ones_ref,
    rows_ref, out_ref, weight_ref, sems,
):
    weight_copy = pltpu.make_async_copy(weight_hbm, weight_ref, sems.at[3])
    weight_copy.start()
    lane = lax.broadcasted_iota(jnp.int32, (1, 256), 1)
    for at, halo_ref in enumerate((halo_first_ref, halo_last_ref)):
        halo = halo_ref[...].astype(f32)
        halo_ones_ref[at] = (jnp.where(lane < 192, halo[:, :256], 1.0) * edge_ref[at]).astype(bf16)
        halo_key_ref[at] = jnp.transpose(halo)[192:].astype(bf16)

    total, least = jnp.zeros((128, 128), f32), jnp.ones((128, 128), f32)
    for tile, own, window, seen in tiles():
        pair = []
        for at, frame in enumerate((0, 3)):
            more = weigh(
                q_ref[frame : frame + 1, own, :],
                halo_key_ref[at, :, window],
                halo_ones_ref[at, window, :],
                mask_ref[tile, :, seen],
            )
            pair.append(
                [
                    part_ref[at, own, 128 * head : 128 * head + 128] + more[head][0]
                    for head in range(3)
                ]
            )
        tile_total, tile_least = put_rows(rows_ref, tile, pair)
        total, least = total + tile_total, jnp.minimum(least, tile_least)
    bad = outside_range(total, least)

    @pl.when(bad > 0.0)
    def _():
        own_frames = [(k_ref.at[g], v_ref.at[g], None) for g in range(4)]
        halos = [(halo_key_ref.at[at], halo_ones_ref.at[at], edge_ref[at]) for at in (0, 1)]
        attend_again(
            q_ref, [(0, own_frames[:2] + halos[:1]), (3, own_frames[2:] + halos[1:])], rows_ref
        )

    here = block_means(rows_ref)
    pairs = here[0] + inner_mean_ref[:, :128]
    third = here[1] + inner_mean_ref[:, 128:]
    third = third + pltpu.roll(third, 64, axis=1)
    weight_copy.wait()
    partial = nn_dot(pairs.astype(bf16), weight_ref[:128, :])
    partial += nn_dot(third[:, :64].astype(bf16), weight_ref[128:, :])
    partial_ref[...] = partial.astype(bf16)
    put_products(rows_ref, first_ref, third_ref, out_ref, out_hbm.at[:, 1], sems)


OUT_SCRATCH = [
    pltpu.VMEM((1, 3 * TOKENS, 128), bf16),
    pltpu.VMEM((4, 3 * TOKENS, 128), bf16),
    pltpu.VMEM((192, 768), bf16),
    pltpu.SemaphoreType.DMA((4,)),
]


def attend_inner(q, k, v, weight):
    vmem, hbm = pl.BlockSpec(memory_space=pltpu.VMEM), pl.BlockSpec(memory_space=pltpu.HBM)
    return pl.pallas_call(
        inner_kernel,
        in_specs=[vmem] * 3 + [hbm],
        out_specs=[hbm] + [vmem] * 5,
        out_shape=[
            pltpu.HBM((4, 2, 3 * TOKENS, 128), bf16),
            jax.ShapeDtypeStruct((4, 128, 384), bf16),
            jax.ShapeDtypeStruct((32, 256), f32),
            jax.ShapeDtypeStruct((2, TOKENS, 384), f32),
            jax.ShapeDtypeStruct((2, 256, 512), bf16),
            jax.ShapeDtypeStruct((384, 512), bf16),
        ],
        scratch_shapes=OUT_SCRATCH,
        compiler_params=params(24),
        cost_estimate=cost(10 * 2 * 512 * 320 * 3 * 256, 6e6, 10 * 512 * 320 * 3),
        name="attend_inner",
    )(q, k, v, *in_hbm(weight))


def attend_outer(
    edge, mask, q, k, v, part, first, last, inner_mean, weight, first_weight, third_weight, inner
):
    vmem, hbm = pl.BlockSpec(memory_space=pltpu.VMEM), pl.BlockSpec(memory_space=pltpu.HBM)
    return pl.pallas_call(
        outer_kernel,
        in_specs=[pl.BlockSpec(memory_space=pltpu.SMEM)] + [vmem] * 10 + [hbm] * 2,
        out_specs=[hbm, vmem],
        out_shape=[
            pltpu.HBM((4, 2, 3 * TOKENS, 128), bf16),
            jax.ShapeDtypeStruct((32, 768), bf16),
        ],
        input_output_aliases={12: 0},
        scratch_shapes=[
            pltpu.VMEM((2, 192, TOKENS), bf16),
            pltpu.VMEM((2, TOKENS, 256), bf16),
        ]
        + OUT_SCRATCH,
        compiler_params=params(24),
        cost_estimate=cost(2 * 2 * 512 * 320 * 3 * 256, 6e6, 2 * 512 * 320 * 3),
        name="attend_outer",
    )(
        edge, mask, q, k, v, part, first, last, inner_mean, first_weight, third_weight,
        *in_hbm(weight), inner,
    )


def load_kernel(_, *refs):
    sources, targets, sems = refs[:4], refs[4:8], refs[8]
    copies = []
    for source, target in zip(sources, targets):
        pieces = [(source, target)]
        if len(source.shape) == 3:
            halves = [(i, pl.ds(768 * half, 768)) for i in range(3) for half in range(2)]
            pieces = [(source.at[i, rows], target.at[i, rows]) for i, rows in halves]
        elif source.shape[0] == 768:
            quarters = [pl.ds(192 * i, 192) for i in range(4)]
            pieces = [(source.at[rows], target.at[rows]) for rows in quarters]
        for here, there in pieces:
            copies.append(pltpu.make_async_copy(here, there, sems.at[len(copies)]))
    for copy in copies:
        copy.start()
    for copy in copies:
        copy.wait()


def load(after, *arrays):
    anywhere = pl.BlockSpec(memory_space=pl.ANY)
    return pl.pallas_call(
        load_kernel,
        in_specs=[anywhere] * 5,
        out_specs=[anywhere] * 4,
        out_shape=[pltpu.VMEM(array.shape, array.dtype) for array in arrays],
        scratch_shapes=[pltpu.SemaphoreType.DMA((12,))],
        compiler_params=params(4),
        cost_estimate=cost(0, 6e6),
        name="load",
    )(after, *in_hbm(*arrays))


def coarse_project_kernel(
    p0, p1, p2, p3, mean_ref, merge_ref, gain_ref, weight_ref, coarse_ref, q_ref, kv_ref
):
    pooled = mean_ref[...] + (
        (p0[...].astype(f32) + p1[...].astype(f32)) + (p2[...].astype(f32) + p3[...].astype(f32))
    )
    coarse = nn_dot(pooled.astype(bf16), merge_ref[...]).astype(bf16)
    coarse_ref[...] = coarse
    wide = coarse.astype(f32)
    scale = lax.rsqrt(jnp.mean(wide * wide, axis=-1, keepdims=True) + EPSILON)
    normed = (wide * scale * gain_ref[...].reshape(1, 1536)).astype(bf16)
    q_ref[...] = (nn_dot(normed, weight_ref[0]) * (128**-0.5 * LOG2E)).astype(bf16)
    key = nn_dot(normed, weight_ref[1]).astype(bf16)
    value = nn_dot(normed, weight_ref[2]).astype(bf16)
    for copy in range(8):
        kv_ref[copy, :, :384] = key
        kv_ref[copy, :, 384:] = value


def coarse_project(partials, mean, merge, gain, weight):
    return pl.pallas_call(
        coarse_project_kernel,
        in_specs=[pl.BlockSpec(memory_space=pltpu.VMEM)] * 8,
        out_specs=[whole(32, 1536), whole(32, 384), whole(8, 32, 768)],
        out_shape=[
            jax.ShapeDtypeStruct((32, 1536), bf16),
            jax.ShapeDtypeStruct((32, 384), bf16),
            pltpu.HBM((8, 32, 768), bf16),
        ],
        compiler_params=params(20),
        cost_estimate=cost(2 * 32 * 1536 * 1920, 7e6),
        name="coarse_project",
    )(*partials, mean, merge, gain, weight)


def coarse_attend_kernel(
    q0, q1, q2, q3, kv_ref, other_ref, split_hbm, o0, o1, o2, o3, split_out, sems
):
    split_copy = pltpu.make_async_copy(split_hbm, split_out, sems.at[0])
    split_copy.start()
    query = jnp.concatenate([ref[...] for ref in (q0, q1, q2, q3)], axis=0)
    outs = (o0, o1, o2, o3)
    lane = lax.broadcasted_iota(jnp.int32, (128, 128), 1)
    stats = jnp.zeros((128, 128), f32)
    for head in range(3):
        lanes = slice(128 * head, 128 * head + 128)
        values = slice(384 + 128 * head, 512 + 128 * head)
        scores = [nt_dot(query[:, lanes], ref[:, lanes]) for ref in (kv_ref, other_ref)]
        top = jnp.max(jnp.maximum(scores[0], scores[1]), axis=-1, keepdims=True)
        weights = [jnp.exp2(score - top) for score in scores]
        total = jnp.sum(weights[0] + weights[1], axis=-1, keepdims=True)
        summed = nn_dot(weights[0].astype(bf16), kv_ref[:, values])
        summed += nn_dot(weights[1].astype(bf16), other_ref[:, values])
        summed = (summed / total).astype(bf16)
        rest = top + jnp.log(total) * LOG2E
        for part in range(3):
            piece = rest.astype(bf16).astype(f32)
            stats = jnp.where(lane == 3 * head + part, piece, stats)
            rest = rest - piece
        for i, out in enumerate(outs):
            out[:, lanes] = summed[32 * i : 32 * i + 32]
    for i, out in enumerate(outs):
        out[:, 384:] = stats[32 * i : 32 * i + 32].astype(bf16)
    split_copy.wait()


def coarse_attend(queries, kv, other, split):
    vmem, anywhere = pl.BlockSpec(memory_space=pltpu.VMEM), pl.BlockSpec(memory_space=pl.ANY)
    return pl.pallas_call(
        coarse_attend_kernel,
        in_specs=[vmem] * 6 + [anywhere],
        out_specs=[vmem] * 4 + [anywhere],
        out_shape=[jax.ShapeDtypeStruct((32, 512), bf16)] * 4 + [pltpu.VMEM(split.shape, bf16)],
        scratch_shapes=[pltpu.SemaphoreType.DMA((1,))],
        compiler_params=params(16),
        cost_estimate=cost(4 * 128 * 512 * 384, 1e6, 128 * 512 * 3),
        name="coarse_attend",
    )(*queries, kv, other, *in_hbm(split))


def coarse_combine_kernel(p0, p1, p2, p3, weight_ref, out_ref):
    parts = (p0, p1, p2, p3)
    heads = []
    for head in range(3):
        lanes = slice(128 * head, 128 * head + 128)
        logs = [
            jnp.sum(part[:, 384 + 3 * head : 387 + 3 * head].astype(f32), axis=-1, keepdims=True)
            for part in parts
        ]
        top = functools.reduce(jnp.maximum, logs)
        shares = [jnp.exp2(log - top) for log in logs]
        summed = sum(share * part[:, lanes].astype(f32) for share, part in zip(shares, parts))
        heads.append((summed / sum(shares)).astype(bf16))
    attended = jnp.concatenate(heads, axis=-1)
    out_ref[...] = nn_dot(attended, weight_ref[...]).astype(bf16)


def coarse_combine(parts, weight):
    return pl.pallas_call(
        coarse_combine_kernel,
        out_shape=jax.ShapeDtypeStruct((32, 1536), bf16),
        compiler_params=params(16),
        cost_estimate=cost(2 * 32 * 384 * 1536, 2e6),
        name="coarse_combine",
    )(*parts, weight)


def split_kernel(
    x_hbm, rows_hbm, coarse_ref, p0, p1, p2, p3, weight_ref, out_hbm,
    x_ref, rows_ref, out_ref, in_sems, out_sems,
):
    x_copies = [
        pltpu.make_async_copy(x_hbm.at[frame], x_ref.at[frame], in_sems.at[2 + frame])
        for frame in range(4)
    ]
    in_copies = [
        pltpu.make_async_copy(rows_hbm.at[pair], rows_ref.at[pair], in_sems.at[pair])
        for pair in (0, 1)
    ]
    for pair, frames in enumerate(((1, 2), (0, 3))):
        in_copies[pair].start()
        for frame in frames:
            x_copies[frame].start()
    mixed = (p0[...].astype(f32) + p1[...].astype(f32)) + (
        p2[...].astype(f32) + p3[...].astype(f32)
    )
    after = (coarse_ref[...].astype(f32) + mixed).astype(bf16)
    split = nt_dot(after, weight_ref[...])
    row = lax.broadcasted_iota(jnp.int32, (128, 32), 0)
    col = lax.broadcasted_iota(jnp.int32, (128, 32), 1)
    spread = jnp.where(col == (row >> 5) * 8 + ((row & 31) >> 2), 1.0, 0.0)
    grid = jnp.dot(spread, split, preferred_element_type=f32, precision=lax.Precision.HIGHEST)
    out_copies = []
    for pair, frames in enumerate(((1, 2), (0, 3))):
        in_copies[pair].wait()
        third = rows_ref[pair, 2 * TOKENS :, :].astype(f32)
        for at, frame in enumerate(frames):
            x_copies[frame].wait()
            x = x_ref[frame].astype(f32)
            one = rows_ref[pair, TOKENS * at : TOKENS * (at + 1), :].astype(f32)
            two = pltpu.roll(third, 64, axis=1) if at else third
            for lanes, added in ((slice(0, 128), one), (slice(128, 192), two[:, :64])):
                hidden = (x[:, lanes] + added).astype(bf16).astype(f32)
                hidden = hidden.reshape(4, 4, COLS, -1) + grid[:, lanes].reshape(4, 1, COLS, -1)
                out_ref[frame, :, :, lanes] = hidden.reshape(ROWS, COLS, -1).astype(bf16)
            out_copies.append(
                pltpu.make_async_copy(out_ref.at[frame], out_hbm.at[frame], out_sems.at[frame])
            )
            out_copies[-1].start()
    for copy in out_copies:
        copy.wait()


def split_rows(x, rows, coarse, partials, weight):
    vmem, hbm = pl.BlockSpec(memory_space=pltpu.VMEM), pl.BlockSpec(memory_space=pltpu.HBM)
    return pl.pallas_call(
        split_kernel,
        in_specs=[hbm, hbm] + [vmem] * 6,
        out_specs=hbm,
        out_shape=jax.ShapeDtypeStruct((4, ROWS, COLS, 192), bf16),
        scratch_shapes=[
            pltpu.VMEM((4, TOKENS, 192), bf16),
            pltpu.VMEM((2, 3 * TOKENS, 128), bf16),
            pltpu.VMEM((4, ROWS, COLS, 192), bf16),
            pltpu.SemaphoreType.DMA((6,)),
            pltpu.SemaphoreType.DMA((4,)),
        ],
        compiler_params=params(24),
        cost_estimate=cost(2 * 32 * 1536 * 192, 4e6),
        name="split_rows",
    )(*in_hbm(x, rows), coarse, *partials, weight)


def shifted(value, axis, shift):
    return lax.ppermute(value, axis, [(i, (i + shift) % 4) for i in range(4)])


def from_others(value, axis):
    return [shifted(value, axis, shift) for shift in (1, 2, 3)]


def body(x, fine_gain, fine_qkv, fine_out, merge, coarse_gain, coarse_qkv, coarse_out, split):
    x = x.reshape(4, TOKENS, 768)
    groups = lax.axis_size(FRAMES)
    here = lax.axis_index(FRAMES)
    place = lax.axis_index("mp").astype(jnp.int32).reshape(1)
    edge = jnp.stack(
        [jnp.where(here == 0, 0.0, 1.0), jnp.where(here == groups - 1, 0.0, 1.0)]
    ).astype(f32)

    q, k, v, initial, final, frame_mean, own = fine_project(
        place, x, fine_gain, jnp.transpose(fine_qkv, (1, 2, 0))
    )
    first = lax.ppermute(final, FRAMES, [(i, i + 1) for i in range(groups - 1)])
    last = lax.ppermute(initial, FRAMES, [(i + 1, i) for i in range(groups - 1)])
    inner, mask, inner_mean, part, *weights = attend_inner(q, k, v, fine_out)
    products, partial = attend_outer(
        edge, mask, q, k, v, part, first, last, inner_mean, fine_out, *weights, inner
    )
    partials = from_others(partial, "mp")
    rows = lax.psum_scatter(products, "mp", scatter_dimension=0, tiled=True)
    frame_mean, merge, coarse_qkv, coarse_gain = load(
        partials[0], frame_mean, merge, jnp.transpose(coarse_qkv, (1, 0, 2)), coarse_gain
    )

    coarse, coarse_q, coarse_kv = coarse_project(
        [partial] + partials, frame_mean, merge, coarse_gain, coarse_qkv
    )
    coarse_kv = lax.all_to_all(coarse_kv, "z", 0, 0, tiled=True).reshape(256, 768)
    queries = [coarse_q] + from_others(coarse_q, "x")
    coarse_kv, queries = lax.optimization_barrier((coarse_kv, queries))
    other_kv = lax.ppermute(coarse_kv, "core", [(0, 1), (1, 0)])
    *parts, split = coarse_attend(queries, coarse_kv, other_kv, jnp.transpose(split, (1, 0)))
    parts = parts[:1] + [shifted(parts[s], "x", 4 - s) for s in (1, 2, 3)]
    coarse_partial = coarse_combine(parts, coarse_out)
    coarse_partials = [coarse_partial] + from_others(coarse_partial, "mp")
    return split_rows(
        own, rows.reshape(2, 3 * TOKENS, 128), coarse, coarse_partials, split
    )


def solution(mesh):
    parts = jax.sharding.Mesh(mesh.devices.reshape(4, 8, 2, 4), FRAMES + ("mp",))
    in_specs = (
        P(FRAMES, None, None, None),
        P(),
        P(None, None, "mp"),
        P("mp", None),
        P(),
        P(),
        P(None, None, "mp"),
        P("mp", None),
        P(None, "mp"),
    )
    out_specs = P(FRAMES, None, None, "mp")
    return jax.shard_map(body, mesh=parts, in_specs=in_specs, out_specs=out_specs, check_vma=False)
```

```python
import functools

import jax
import jax.numpy as jnp
from jax import lax
from jax.experimental import pallas as pl
from jax.experimental.pallas import tpu as pltpu
from jax.sharding import PartitionSpec as P

HEADS = 12
EPSILON = 1e-06
REACH = 3
LOG2E = 1.4426950408889634
ROWS, COLS = 16, 32
TOKENS = ROWS * COLS
FRAMES = ("x", "z", "core")
MIB = 1 << 20
bf16, f32 = jnp.bfloat16, jnp.float32


def nt_dot(a, b):
    return lax.dot_general(a, b, (((1,), (1,)), ((), ())), preferred_element_type=f32)


def nn_dot(a, b):
    return jnp.dot(a, b, preferred_element_type=f32)


def block_mean_matrix(rows):
    token = lax.broadcasted_iota(jnp.int32, (32, rows * COLS), 1)
    block = lax.broadcasted_iota(jnp.int32, (32, rows * COLS), 0)
    of_token = token // (rows * COLS // 4) * 8 + ((token & 31) >> 2)
    return jnp.where(of_token == block, 1.0 / 64, 0.0)


def params(mib):
    return pltpu.CompilerParams(vmem_limit_bytes=mib * MIB)


def cost(flops, bytes_accessed, transcendentals=0):
    return pl.CostEstimate(
        flops=int(flops), bytes_accessed=int(bytes_accessed), transcendentals=int(transcendentals)
    )


def whole(*shape):
    return pl.BlockSpec(shape, lambda *i: (0,) * len(shape))


def fine_project_kernel(
    place_ref, x_hbm, gain_hbm, weight_hbm,
    q_ref, key_ref, ones_ref, initial_hbm, last_hbm, mean_hbm, own_hbm,
    x_ref, gain_ref, weight_ref, rows_ref, sum_ref, edge_ref, own_ref, mean_ref,
    in_sems, out_sems,
):
    gain_copy = pltpu.make_async_copy(gain_hbm, gain_ref, in_sems.at[5])
    gain_copy.start()
    weight_copy = pltpu.make_async_copy(weight_hbm, weight_ref, in_sems.at[4])
    weight_copy.start()
    x_copies = [
        pltpu.make_async_copy(x_hbm.at[frame], x_ref.at[frame], in_sems.at[frame])
        for frame in range(4)
    ]
    order = (0, 3, 1, 2)
    for frame in order:
        x_copies[frame].start()
    gain_copy.wait()
    weight_copy.wait()
    gain = gain_ref[...].reshape(1, 768)
    query, key, value = (weight_ref[i].astype(f32) * gain for i in range(3))
    rows_ref[:192, :] = value.astype(bf16)
    rows_ref[192:384, :] = key.astype(bf16)
    rows_ref[384:, :] = (query * (0.125 * LOG2E)).astype(bf16)

    out_copies = [
        pltpu.make_async_copy(edge_ref.at[i], out, out_sems.at[i])
        for i, out in enumerate((initial_hbm, last_hbm))
    ]

    for step, frame in enumerate(order):
        x_copies[frame].wait()
        if step == 3:
            for place in range(4):

                @pl.when(place_ref[0] == place)
                def _():
                    own_ref[...] = x_ref[:, :, 192 * place : 192 * place + 192]

            out_copies.append(pltpu.make_async_copy(own_ref, own_hbm, out_sems.at[2]))
            out_copies[-1].start()
        x = x_ref[frame]
        wide = x.astype(f32)
        added = jnp.sum(wide.reshape(4, 4, COLS, 768), axis=1).reshape(4 * COLS, 768)
        sum_ref[...] = sum_ref[...] + added if step else added
        if step == 3:
            mean_ref[...] = jnp.dot(
                block_mean_matrix(4),
                sum_ref[...],
                preferred_element_type=f32,
                precision=lax.Precision.HIGHEST,
            )
            out_copies.append(pltpu.make_async_copy(mean_ref, mean_hbm, out_sems.at[3]))
            out_copies[-1].start()
        projected = nt_dot(x, rows_ref[...])
        scale = lax.rsqrt(jnp.mean(wide * wide, axis=-1, keepdims=True) + EPSILON)
        projected = projected * scale
        q_ref[frame] = projected[:, 384:].astype(bf16)
        pairs = projected[:, :384]
        lane = lax.broadcasted_iota(jnp.int32, (1, 256), 1)
        ones_ref[frame] = jnp.where(lane < 192, projected[:, :256], 1.0).astype(bf16)
        along = jnp.transpose(jnp.broadcast_to(scale, (TOKENS, 128)))[:1]
        key_ref[frame] = (nt_dot(rows_ref[192:384, :], x) * along).astype(bf16)
        if step < 2:
            edge_ref[step] = pairs.astype(bf16)
            out_copies[step].start()
    for copy in out_copies:
        copy.wait()


def in_hbm(*arrays):
    return [pltpu.with_memory_space_constraint(array, pltpu.HBM) for array in arrays]


def fine_project(place, x, gain, weight):
    vmem, hbm = pl.BlockSpec(memory_space=pltpu.VMEM), pl.BlockSpec(memory_space=pltpu.HBM)
    return pl.pallas_call(
        fine_project_kernel,
        in_specs=[pl.BlockSpec(memory_space=pltpu.SMEM), hbm, hbm, hbm],
        out_specs=[vmem, vmem, vmem, hbm, hbm, hbm, hbm],
        out_shape=[
            jax.ShapeDtypeStruct((4, TOKENS, 192), bf16),
            jax.ShapeDtypeStruct((4, 192, TOKENS), bf16),
            jax.ShapeDtypeStruct((4, TOKENS, 256), bf16),
            pltpu.HBM((TOKENS, 384), bf16),
            pltpu.HBM((TOKENS, 384), bf16),
            pltpu.HBM((32, 768), f32),
            pltpu.HBM((4, TOKENS, 192), bf16),
        ],
        scratch_shapes=[
            pltpu.VMEM((4, TOKENS, 768), bf16),
            pltpu.VMEM((768,), f32),
            pltpu.VMEM((3, 192, 768), bf16),
            pltpu.VMEM((576, 768), bf16),
            pltpu.VMEM((128, 768), f32),
            pltpu.VMEM((2, TOKENS, 384), bf16),
            pltpu.VMEM((4, TOKENS, 192), bf16),
            pltpu.VMEM((32, 768), f32),
            pltpu.SemaphoreType.DMA((6,)),
            pltpu.SemaphoreType.DMA((4,)),
        ],
        compiler_params=params(24),
        cost_estimate=cost(2 * 2048 * 768 * 768, 8e6),
        name="fine_project",
    )(place, *in_hbm(x, gain, weight))


BASES = (0, 0, 128, 128)
WINDOWS = ((0, 256), (0, 384), (128, 512), (256, 512))


def near_keys(tile, base):
    query = lax.broadcasted_iota(jnp.int32, (128, 384), 0) + 128 * tile
    key = lax.broadcasted_iota(jnp.int32, (128, 384), 1) + base
    rows = jnp.abs((query >> 5) - (key >> 5))
    cols = jnp.abs((query & 31) - (key & 31))
    return (rows <= REACH) & (cols <= REACH)


def outside_range(total, least):
    low = lax.broadcasted_iota(jnp.int32, (128, 128), 1) < 64
    bad = jnp.where((total < 2.0**60) & (least > 2.0**-60), 0.0, 1.0)
    return jnp.max(jnp.where(low, bad, 0.0))


def rows_at(part, tile):
    start = part * TOKENS + tile * 128
    return pl.ds(start if isinstance(start, int) else pl.multiple_of(start, 128), 128)


def window_of(tile):
    base = pl.multiple_of((tile >> 1) * 128, 128)
    return base, pl.ds(base, 384), pl.ds(pl.multiple_of(tile * 128, 128), 128)


def put_rows(out_ref, tile, pair):
    low = lax.broadcasted_iota(jnp.int32, (128, 128), 1) < 64
    thirds, counts = [], []
    for at, sums in enumerate(pair):
        turned = [pltpu.roll(one, 64, axis=1) for one in sums]
        heads = [one / other for one, other in zip(sums, turned)]
        out_ref[0, rows_at(at, tile), :] = jnp.where(
            low, heads[0], heads[1]
        ).astype(bf16)
        thirds.append(heads[2])
        counts += [turned[0], sums[1], turned[2]]
    packed = jnp.where(low, thirds[0], pltpu.roll(thirds[1], 64, axis=1))
    out_ref[0, rows_at(2, tile), :] = packed.astype(bf16)
    return sum(counts), functools.reduce(jnp.minimum, counts)


def stack_heads(query):
    head = lax.broadcasted_iota(jnp.int32, (1, 192), 1) >> 6
    return jnp.concatenate(
        [query * jnp.where(head == i, 1.0, 0.0).astype(bf16) for i in range(3)], axis=0
    )


def own_parts(summed):
    low = lax.broadcasted_iota(jnp.int32, (1, 128, 128), 2) < 64
    first, second = summed[..., :128], summed[..., 128:]
    n = summed.shape[1]
    turned = pltpu.roll(second[1].reshape(n * 128, 128), 64, axis=1).reshape(n, 128, 128)
    return [
        jnp.where(low, first[0], second[0]),
        jnp.where(low, turned, first[1]),
        second[2],
    ]


def attend_again(q_ref, frames, out_ref):
    def redo(tile, _):
        base, window, own = window_of(tile)
        near = jnp.concatenate([near_keys(tile, base)] * 3, axis=0)
        pair = []
        for frame, sources in frames:
            query = stack_heads(q_ref[frame, own, :])
            scores = []
            for keys, _, inside in sources:
                seen = near if inside is None else near & (inside > 0.0)
                scores.append(jnp.where(seen, nn_dot(query, keys[:, window]), -jnp.inf))
            top = jnp.max(
                jnp.maximum(jnp.maximum(scores[0], scores[1]), scores[2]), axis=-1, keepdims=True
            )
            summed = sum(
                nn_dot(jnp.exp2(score - top).astype(bf16), ones[window, :])
                for score, (_, ones, _) in zip(scores, sources)
            )
            pair.append([part[0] for part in own_parts(summed.reshape(3, 1, 128, 256))])
        put_rows(out_ref, tile, pair)
        return 0

    lax.fori_loop(0, 4, redo, 0)


def weigh(query, keys, ones, mask):
    n = query.shape[0]
    weights = jnp.exp2(nn_dot(stack_heads(query.reshape(n * 128, 192)), keys)).astype(bf16)
    weights = (weights.reshape(3 * n, *mask.shape) * mask[None]).reshape(-1, mask.shape[1])
    return own_parts(nn_dot(weights, ones).reshape(3, n, 128, 256))


def tiles():
    for tile in range(4):
        first, last = WINDOWS[tile]
        own = slice(128 * tile, 128 * tile + 128)
        yield tile, own, slice(first, last), slice(first - BASES[tile], last - BASES[tile])


def block_means(out_ref):
    matrix = block_mean_matrix(ROWS).astype(bf16)
    pairs = nn_dot(matrix, out_ref[0, :TOKENS, :])
    pairs += nn_dot(matrix, out_ref[0, TOKENS : 2 * TOKENS, :])
    return pairs, nn_dot(matrix, out_ref[0, 2 * TOKENS :, :])


def set_weights(weight_ref, first_ref, third_ref):
    first_ref[...] = jnp.zeros_like(first_ref)
    third_ref[...] = jnp.zeros_like(third_ref)
    for place in range(4):
        weight = weight_ref[:, 192 * place : 192 * place + 192]
        lanes = slice(128 * place, 128 * place + 128)
        for at in (0, 1):
            first_ref[at, :128, lanes] = weight[:128, :128]
            first_ref[at, 128 + 64 * at : 192 + 64 * at, lanes] = weight[128:, :128]
            half = slice(128 * place + 64 * at, 128 * place + 64 * at + 64)
            third_ref[128 * at : 128 * at + 128, half] = weight[:128, 128:]
            third_ref[256 + 64 * at : 320 + 64 * at, half] = weight[128:, 128:]


def put_products(rows_ref, first_ref, third_ref, out_ref, out_hbm, sems):
    parts = [rows_ref[0, TOKENS * i : TOKENS * (i + 1), :] for i in range(3)]
    copies = []
    for i in range(3):
        if i < 2:
            product = nn_dot(jnp.concatenate([parts[i], parts[2]], axis=1), first_ref[i])
        else:
            product = nn_dot(jnp.concatenate(parts, axis=1), third_ref[...])
        own = pl.ds(TOKENS * i, TOKENS)
        for place in range(4):
            out_ref[place, own, :] = product[:, 128 * place : 128 * place + 128].astype(bf16)
        copies.append(
            pltpu.make_async_copy(out_ref.at[:, own, :], out_hbm.at[:, own, :], sems.at[i])
        )
        copies[-1].start()
    for copy in copies:
        copy.wait()


def inner_kernel(
    q_ref, k_ref, v_ref, weight_hbm,
    out_hbm, mask_ref, mean_ref, part_ref, first_ref, third_ref, rows_ref, out_ref, weight_ref, sems,
):
    weight_copy = pltpu.make_async_copy(weight_hbm, weight_ref, sems.at[3])
    weight_copy.start()

    total, least = jnp.zeros((128, 128), f32), jnp.ones((128, 128), f32)
    for tile, own, window, seen in tiles():
        mask_ref[tile] = jnp.where(near_keys(tile, BASES[tile]), 1.0, 0.0).astype(bf16)
        sums = [None] * 4
        for g in range(4):
            lo, hi = max(g - 1, 0), min(g + 1, 3)
            parts = weigh(
                q_ref[lo : hi + 1, own, :],
                k_ref[g, :, window],
                v_ref[g, window, :],
                mask_ref[tile, :, seen],
            )
            for f in range(lo, hi + 1):
                here = [part[f - lo] for part in parts]
                sums[f] = here if sums[f] is None else [a + b for a, b in zip(sums[f], here)]
        for head in range(3):
            lanes = slice(128 * head, 128 * head + 128)
            part_ref[0, own, lanes] = sums[0][head]
            part_ref[1, own, lanes] = sums[3][head]
        tile_total, tile_least = put_rows(rows_ref, tile, sums[1:3])
        total, least = total + tile_total, jnp.minimum(least, tile_least)
    bad = outside_range(total, least)

    @pl.when(bad > 0.0)
    def _():
        own_frames = [(k_ref.at[g], v_ref.at[g], None) for g in range(4)]
        attend_again(q_ref, [(1, own_frames[:3]), (2, own_frames[1:])], rows_ref)

    mean_ref[:, :128], mean_ref[:, 128:] = block_means(rows_ref)
    weight_copy.wait()
    set_weights(weight_ref, first_ref, third_ref)
    put_products(rows_ref, first_ref, third_ref, out_ref, out_hbm.at[:, 0], sems)


def outer_kernel(
    edge_ref, mask_ref, q_ref, k_ref, v_ref, part_ref, halo_first_ref, halo_last_ref,
    inner_mean_ref, first_ref, third_ref, weight_hbm, inner_ref,
    out_hbm, partial_ref, halo_key_ref, halo_ones_ref,
    rows_ref, out_ref, weight_ref, sems,
):
    weight_copy = pltpu.make_async_copy(weight_hbm, weight_ref, sems.at[3])
    weight_copy.start()
    lane = lax.broadcasted_iota(jnp.int32, (1, 256), 1)
    for at, halo_ref in enumerate((halo_first_ref, halo_last_ref)):
        halo = halo_ref[...].astype(f32)
        halo_ones_ref[at] = (jnp.where(lane < 192, halo[:, :256], 1.0) * edge_ref[at]).astype(bf16)
        halo_key_ref[at] = jnp.transpose(halo)[192:].astype(bf16)

    total, least = jnp.zeros((128, 128), f32), jnp.ones((128, 128), f32)
    for tile, own, window, seen in tiles():
        pair = []
        for at, frame in enumerate((0, 3)):
            more = weigh(
                q_ref[frame : frame + 1, own, :],
                halo_key_ref[at, :, window],
                halo_ones_ref[at, window, :],
                mask_ref[tile, :, seen],
            )
            pair.append(
                [
                    part_ref[at, own, 128 * head : 128 * head + 128] + more[head][0]
                    for head in range(3)
                ]
            )
        tile_total, tile_least = put_rows(rows_ref, tile, pair)
        total, least = total + tile_total, jnp.minimum(least, tile_least)
    bad = outside_range(total, least)

    @pl.when(bad > 0.0)
    def _():
        own_frames = [(k_ref.at[g], v_ref.at[g], None) for g in range(4)]
        halos = [(halo_key_ref.at[at], halo_ones_ref.at[at], edge_ref[at]) for at in (0, 1)]
        attend_again(
            q_ref, [(0, own_frames[:2] + halos[:1]), (3, own_frames[2:] + halos[1:])], rows_ref
        )

    here = block_means(rows_ref)
    pairs = here[0] + inner_mean_ref[:, :128]
    third = here[1] + inner_mean_ref[:, 128:]
    third = third + pltpu.roll(third, 64, axis=1)
    weight_copy.wait()
    partial = nn_dot(pairs.astype(bf16), weight_ref[:128, :])
    partial += nn_dot(third[:, :64].astype(bf16), weight_ref[128:, :])
    partial_ref[...] = partial.astype(bf16)
    put_products(rows_ref, first_ref, third_ref, out_ref, out_hbm.at[:, 1], sems)


OUT_SCRATCH = [
    pltpu.VMEM((1, 3 * TOKENS, 128), bf16),
    pltpu.VMEM((4, 3 * TOKENS, 128), bf16),
    pltpu.VMEM((192, 768), bf16),
    pltpu.SemaphoreType.DMA((4,)),
]


def attend_inner(q, k, v, weight):
    vmem, hbm = pl.BlockSpec(memory_space=pltpu.VMEM), pl.BlockSpec(memory_space=pltpu.HBM)
    return pl.pallas_call(
        inner_kernel,
        in_specs=[vmem] * 3 + [hbm],
        out_specs=[hbm] + [vmem] * 5,
        out_shape=[
            pltpu.HBM((4, 2, 3 * TOKENS, 128), bf16),
            jax.ShapeDtypeStruct((4, 128, 384), bf16),
            jax.ShapeDtypeStruct((32, 256), f32),
            jax.ShapeDtypeStruct((2, TOKENS, 384), f32),
            jax.ShapeDtypeStruct((2, 256, 512), bf16),
            jax.ShapeDtypeStruct((384, 512), bf16),
        ],
        scratch_shapes=OUT_SCRATCH,
        compiler_params=params(24),
        cost_estimate=cost(10 * 2 * 512 * 320 * 3 * 256, 6e6, 10 * 512 * 320 * 3),
        name="attend_inner",
    )(q, k, v, *in_hbm(weight))


def attend_outer(
    edge, mask, q, k, v, part, first, last, inner_mean, weight, first_weight, third_weight, inner
):
    vmem, hbm = pl.BlockSpec(memory_space=pltpu.VMEM), pl.BlockSpec(memory_space=pltpu.HBM)
    return pl.pallas_call(
        outer_kernel,
        in_specs=[pl.BlockSpec(memory_space=pltpu.SMEM)] + [vmem] * 10 + [hbm] * 2,
        out_specs=[hbm, vmem],
        out_shape=[
            pltpu.HBM((4, 2, 3 * TOKENS, 128), bf16),
            jax.ShapeDtypeStruct((32, 768), bf16),
        ],
        input_output_aliases={12: 0},
        scratch_shapes=[
            pltpu.VMEM((2, 192, TOKENS), bf16),
            pltpu.VMEM((2, TOKENS, 256), bf16),
        ]
        + OUT_SCRATCH,
        compiler_params=params(24),
        cost_estimate=cost(2 * 2 * 512 * 320 * 3 * 256, 6e6, 2 * 512 * 320 * 3),
        name="attend_outer",
    )(
        edge, mask, q, k, v, part, first, last, inner_mean, first_weight, third_weight,
        *in_hbm(weight), inner,
    )


def load_kernel(_, *refs):
    sources, targets, sems = refs[:4], refs[4:8], refs[8]
    copies = [
        pltpu.make_async_copy(source, target, sems.at[i])
        for i, (source, target) in enumerate(zip(sources, targets))
    ]
    for copy in copies:
        copy.start()
    for copy in copies:
        copy.wait()


def load(after, *arrays):
    anywhere = pl.BlockSpec(memory_space=pl.ANY)
    return pl.pallas_call(
        load_kernel,
        in_specs=[anywhere] * 5,
        out_specs=[anywhere] * 4,
        out_shape=[pltpu.VMEM(array.shape, array.dtype) for array in arrays],
        scratch_shapes=[pltpu.SemaphoreType.DMA((4,))],
        compiler_params=params(4),
        cost_estimate=cost(0, 6e6),
        name="load",
    )(after, *in_hbm(*arrays))


def coarse_project_kernel(
    p0, p1, p2, p3, mean_ref, merge_ref, gain_ref, weight_ref, coarse_ref, q_ref, kv_ref
):
    pooled = mean_ref[...] + (
        (p0[...].astype(f32) + p1[...].astype(f32)) + (p2[...].astype(f32) + p3[...].astype(f32))
    )
    coarse = nn_dot(pooled.astype(bf16), merge_ref[...]).astype(bf16)
    coarse_ref[...] = coarse
    wide = coarse.astype(f32)
    scale = lax.rsqrt(jnp.mean(wide * wide, axis=-1, keepdims=True) + EPSILON)
    normed = (wide * scale * gain_ref[...].reshape(1, 1536)).astype(bf16)
    q_ref[...] = (nn_dot(normed, weight_ref[0]) * (128**-0.5 * LOG2E)).astype(bf16)
    key = nn_dot(normed, weight_ref[1]).astype(bf16)
    value = nn_dot(normed, weight_ref[2]).astype(bf16)
    for copy in range(8):
        kv_ref[copy, :, :384] = key
        kv_ref[copy, :, 384:] = value


def coarse_project(partials, mean, merge, gain, weight):
    return pl.pallas_call(
        coarse_project_kernel,
        in_specs=[pl.BlockSpec(memory_space=pltpu.VMEM)] * 8,
        out_specs=[whole(32, 1536), whole(32, 384), whole(8, 32, 768)],
        out_shape=[
            jax.ShapeDtypeStruct((32, 1536), bf16),
            jax.ShapeDtypeStruct((32, 384), bf16),
            pltpu.HBM((8, 32, 768), bf16),
        ],
        compiler_params=params(20),
        cost_estimate=cost(2 * 32 * 1536 * 1920, 7e6),
        name="coarse_project",
    )(*partials, mean, merge, gain, weight)


def coarse_attend_kernel(
    q0, q1, q2, q3, kv_ref, other_ref, split_hbm, o0, o1, o2, o3, split_out, sems
):
    split_copy = pltpu.make_async_copy(split_hbm, split_out, sems.at[0])
    split_copy.start()
    query = jnp.concatenate([ref[...] for ref in (q0, q1, q2, q3)], axis=0)
    outs = (o0, o1, o2, o3)
    lane = lax.broadcasted_iota(jnp.int32, (128, 128), 1)
    stats = jnp.zeros((128, 128), f32)
    for head in range(3):
        lanes = slice(128 * head, 128 * head + 128)
        values = slice(384 + 128 * head, 512 + 128 * head)
        scores = [nt_dot(query[:, lanes], ref[:, lanes]) for ref in (kv_ref, other_ref)]
        top = jnp.max(jnp.maximum(scores[0], scores[1]), axis=-1, keepdims=True)
        weights = [jnp.exp2(score - top) for score in scores]
        total = jnp.sum(weights[0] + weights[1], axis=-1, keepdims=True)
        summed = nn_dot(weights[0].astype(bf16), kv_ref[:, values])
        summed += nn_dot(weights[1].astype(bf16), other_ref[:, values])
        summed = (summed / total).astype(bf16)
        rest = top + jnp.log(total) * LOG2E
        for part in range(3):
            piece = rest.astype(bf16).astype(f32)
            stats = jnp.where(lane == 3 * head + part, piece, stats)
            rest = rest - piece
        for i, out in enumerate(outs):
            out[:, lanes] = summed[32 * i : 32 * i + 32]
    for i, out in enumerate(outs):
        out[:, 384:] = stats[32 * i : 32 * i + 32].astype(bf16)
    split_copy.wait()


def coarse_attend(queries, kv, other, split):
    vmem, anywhere = pl.BlockSpec(memory_space=pltpu.VMEM), pl.BlockSpec(memory_space=pl.ANY)
    return pl.pallas_call(
        coarse_attend_kernel,
        in_specs=[vmem] * 6 + [anywhere],
        out_specs=[vmem] * 4 + [anywhere],
        out_shape=[jax.ShapeDtypeStruct((32, 512), bf16)] * 4 + [pltpu.VMEM(split.shape, bf16)],
        scratch_shapes=[pltpu.SemaphoreType.DMA((1,))],
        compiler_params=params(16),
        cost_estimate=cost(4 * 128 * 512 * 384, 1e6, 128 * 512 * 3),
        name="coarse_attend",
    )(*queries, kv, other, *in_hbm(split))


def coarse_combine_kernel(p0, p1, p2, p3, weight_ref, out_ref):
    parts = (p0, p1, p2, p3)
    heads = []
    for head in range(3):
        lanes = slice(128 * head, 128 * head + 128)
        logs = [
            jnp.sum(part[:, 384 + 3 * head : 387 + 3 * head].astype(f32), axis=-1, keepdims=True)
            for part in parts
        ]
        top = functools.reduce(jnp.maximum, logs)
        shares = [jnp.exp2(log - top) for log in logs]
        summed = sum(share * part[:, lanes].astype(f32) for share, part in zip(shares, parts))
        heads.append((summed / sum(shares)).astype(bf16))
    attended = jnp.concatenate(heads, axis=-1)
    out_ref[...] = nn_dot(attended, weight_ref[...]).astype(bf16)


def coarse_combine(parts, weight):
    return pl.pallas_call(
        coarse_combine_kernel,
        out_shape=jax.ShapeDtypeStruct((32, 1536), bf16),
        compiler_params=params(16),
        cost_estimate=cost(2 * 32 * 384 * 1536, 2e6),
        name="coarse_combine",
    )(*parts, weight)


def split_kernel(
    x_hbm, rows_hbm, coarse_ref, p0, p1, p2, p3, weight_ref, out_hbm,
    x_ref, rows_ref, out_ref, in_sems, out_sems,
):
    x_copy = pltpu.make_async_copy(x_hbm, x_ref, in_sems.at[2])
    x_copy.start()
    in_copies = [
        pltpu.make_async_copy(rows_hbm.at[pair], rows_ref.at[pair], in_sems.at[pair])
        for pair in (0, 1)
    ]
    for copy in in_copies:
        copy.start()
    mixed = (p0[...].astype(f32) + p1[...].astype(f32)) + (
        p2[...].astype(f32) + p3[...].astype(f32)
    )
    after = (coarse_ref[...].astype(f32) + mixed).astype(bf16)
    split = nt_dot(after, weight_ref[...])
    row = lax.broadcasted_iota(jnp.int32, (128, 32), 0)
    col = lax.broadcasted_iota(jnp.int32, (128, 32), 1)
    spread = jnp.where(col == (row >> 5) * 8 + ((row & 31) >> 2), 1.0, 0.0)
    grid = jnp.dot(spread, split, preferred_element_type=f32, precision=lax.Precision.HIGHEST)
    out_copies = []
    x_copy.wait()
    for pair, frames in enumerate(((1, 2), (0, 3))):
        in_copies[pair].wait()
        third = rows_ref[pair, 2 * TOKENS :, :].astype(f32)
        for at, frame in enumerate(frames):
            x = x_ref[frame].astype(f32)
            one = rows_ref[pair, TOKENS * at : TOKENS * (at + 1), :].astype(f32)
            two = pltpu.roll(third, 64, axis=1) if at else third
            for lanes, added in ((slice(0, 128), one), (slice(128, 192), two[:, :64])):
                hidden = (x[:, lanes] + added).astype(bf16).astype(f32)
                hidden = hidden.reshape(4, 4, COLS, -1) + grid[:, lanes].reshape(4, 1, COLS, -1)
                out_ref[frame, :, :, lanes] = hidden.reshape(ROWS, COLS, -1).astype(bf16)
            out_copies.append(
                pltpu.make_async_copy(out_ref.at[frame], out_hbm.at[frame], out_sems.at[frame])
            )
            out_copies[-1].start()
    for copy in out_copies:
        copy.wait()


def split_rows(x, rows, coarse, partials, weight):
    vmem, hbm = pl.BlockSpec(memory_space=pltpu.VMEM), pl.BlockSpec(memory_space=pltpu.HBM)
    return pl.pallas_call(
        split_kernel,
        in_specs=[hbm, hbm] + [vmem] * 6,
        out_specs=hbm,
        out_shape=jax.ShapeDtypeStruct((4, ROWS, COLS, 192), bf16),
        scratch_shapes=[
            pltpu.VMEM((4, TOKENS, 192), bf16),
            pltpu.VMEM((2, 3 * TOKENS, 128), bf16),
            pltpu.VMEM((4, ROWS, COLS, 192), bf16),
            pltpu.SemaphoreType.DMA((3,)),
            pltpu.SemaphoreType.DMA((4,)),
        ],
        compiler_params=params(24),
        cost_estimate=cost(2 * 32 * 1536 * 192, 4e6),
        name="split_rows",
    )(*in_hbm(x, rows), coarse, *partials, weight)


def shifted(value, axis, shift):
    return lax.ppermute(value, axis, [(i, (i + shift) % 4) for i in range(4)])


def from_others(value, axis):
    second = shifted(value, axis, 2)
    return [shifted(value, axis, 1), second, shifted(value, axis, 3)]


def body(x, fine_gain, fine_qkv, fine_out, merge, coarse_gain, coarse_qkv, coarse_out, split):
    x = x.reshape(4, TOKENS, 768)
    groups = lax.axis_size(FRAMES)
    here = lax.axis_index(FRAMES)
    place = lax.axis_index("mp").astype(jnp.int32).reshape(1)
    edge = jnp.stack(
        [jnp.where(here == 0, 0.0, 1.0), jnp.where(here == groups - 1, 0.0, 1.0)]
    ).astype(f32)

    q, k, v, initial, final, frame_mean, own = fine_project(
        place, x, fine_gain, jnp.transpose(fine_qkv, (1, 2, 0))
    )
    first = lax.ppermute(final, FRAMES, [(i, i + 1) for i in range(groups - 1)])
    last = lax.ppermute(initial, FRAMES, [(i + 1, i) for i in range(groups - 1)])
    inner, mask, inner_mean, part, *weights = attend_inner(q, k, v, fine_out)
    products, partial = attend_outer(
        edge, mask, q, k, v, part, first, last, inner_mean, fine_out, *weights, inner
    )
    partials = from_others(partial, "mp")
    rows = lax.psum_scatter(products, "mp", scatter_dimension=0, tiled=True)
    frame_mean, merge, coarse_qkv, coarse_gain = load(
        partials[0], frame_mean, merge, jnp.transpose(coarse_qkv, (1, 0, 2)), coarse_gain
    )

    coarse, coarse_q, coarse_kv = coarse_project(
        [partial] + partials, frame_mean, merge, coarse_gain, coarse_qkv
    )
    coarse_kv = lax.all_to_all(coarse_kv, "z", 0, 0, tiled=True).reshape(256, 768)
    queries = [coarse_q] + from_others(coarse_q, "x")
    coarse_kv, queries = lax.optimization_barrier((coarse_kv, queries))
    other_kv = lax.ppermute(coarse_kv, "core", [(0, 1), (1, 0)])
    *parts, split = coarse_attend(queries, coarse_kv, other_kv, jnp.transpose(split, (1, 0)))
    parts = parts[:1] + [shifted(parts[s], "x", 4 - s) for s in (2, 1, 3)]
    coarse_partial = coarse_combine(parts, coarse_out)
    coarse_partials = [coarse_partial] + from_others(coarse_partial, "mp")
    return split_rows(
        own, rows.reshape(2, 3 * TOKENS, 128), coarse, coarse_partials, split
    )


def solution(mesh):
    parts = jax.sharding.Mesh(mesh.devices.reshape(4, 8, 2, 4), FRAMES + ("mp",))
    in_specs = (
        P(FRAMES, None, None, None),
        P(),
        P(None, None, "mp"),
        P("mp", None),
        P(),
        P(),
        P(None, None, "mp"),
        P("mp", None),
        P(None, "mp"),
    )
    out_specs = P(FRAMES, None, None, "mp")
    return jax.shard_map(body, mesh=parts, in_specs=in_specs, out_specs=out_specs, check_vma=False)
```
